512 devices in a mesh: tm: 32 (over y, x), tile: 16 (over z, core).
Axes of the slice: x: 4, y: 8, z: 8, core: 2. Of those that a mesh axis runs over, the one named last changes fastest.
Arguments:
- latents: bfloat16 [128, 64, 16, 384], P('tm', 'tile'), may hold values from -24 to 24
- first_gain: float32 [384], replicated, may hold values from 0.25 to 1.75
- first_bias: float32 [384], replicated, may hold values from -0.5 to 0.5
- first_kernel: bfloat16 [384, 3, 3, 3, 192], P('tile'), may hold values from -0.0625 to 0.0625
- second_gain: float32 [192], replicated, may hold values from 0.25 to 1.75
- second_bias: float32 [192], replicated, may hold values from -0.5 to 0.5
- second_kernel: bfloat16 [192, 3, 3, 3, 192], replicated, may hold values from -0.078125 to 0.078125
- skip_weight: bfloat16 [384, 192], replicated, may hold values from -0.3125 to 0.3125
- resample_kernel: bfloat16 [3, 3, 192, 96], replicated, may hold values from -0.15625 to 0.15625
- clip_spans: int32 [4], replicated, may hold values from 1 to 16, 32 in all
Outputs:
- upsampled: bfloat16 [128, 128, 16, 192], P('tm', 'tile')
The draws below stay inside these ranges and needn't reach their ends.
All inputs are finite; a program needn't handle non-finite values.
Results may differ from the reference program's by a relative error of at most 0.0059.
Values may be sent and summed in bfloat16 or wider, within the bound.
A program may use at most 64 MiB of HBM per device.

```python
import math
from functools import partial
import jax
import jax.numpy as jnp
import numpy as np
from jax import lax

C_IN = 384
C_MID = 192
C_OUT = 96
GROUPS = 32
CF = 4
WIDTH = 16
CLIPS = 4
SPANS = 32
MOST_CLIP = 16
FRAMES = 128
HEIGHT = 64


def draw_latents(key, part):
    key = jax.random.fold_in(key, 11)
    keys = jax.random.split(key, 3)
    shape = (FRAMES, HEIGHT, WIDTH, C_IN)
    row_scale = jnp.exp(jax.random.uniform(keys[0], (FRAMES, HEIGHT, 1, 1), jnp.float32, math.log(0.3), math.log(3.0)))
    chan_scale = jnp.exp(jax.random.uniform(keys[1], (1, 1, 1, C_IN), jnp.float32, math.log(0.5), math.log(2.0)))
    noise = jax.random.truncated_normal(keys[2], -4.0, 4.0, shape, jnp.float32)
    return (noise * row_scale * chan_scale).astype(jnp.bfloat16)


def steps_of(stream_key, shape, pieces, smallest, top_value):
    def one(axis_at, shards_of):
        heights = jax.random.uniform(jax.random.fold_in(jax.random.fold_in(stream_key, 6), axis_at), (shards_of,), jnp.float32, smallest / len(pieces), top_value / len(pieces))
        return jnp.repeat(jnp.exp(heights), shape[axis_at] // shards_of).reshape((-1,) + (1,) * (len(shape) - axis_at - 1))

    gain = one(*pieces[0])
    for cut in pieces[1:]:
        gain = gain * one(*cut)
    return gain


def split_up(number_of, total, bound, skew):
    portions = [(1 << 20) // math.isqrt(grade ** skew) + 1 for grade in range(2, number_of + 1)]
    spare, holding = total - bound - (number_of - 1), [1] * (number_of - 1)
    while spare > 0:
        movable = [i for i in range(number_of - 1) if holding[i] < bound]
        whole, budget = sum([portions[i] for i in movable]), spare
        for i in movable:
            addition = min(bound - holding[i], max(1, budget * portions[i] // whole), spare)
            holding[i] = holding[i] + addition
            spare = spare - addition
    return np.array([bound] + holding)


def uneven(stream_key, number_of, total, most, skew):
    if number_of == 2:
        one = jax.random.randint(stream_key, (), max(1, total - most), min(most, total - 1) + 1)
        return jnp.stack([one, total - one])
    tallies = jnp.asarray(split_up(number_of, total, most, skew), jnp.int32)
    twos = (number_of - 1) // 2
    source_of, taker = tallies[1:1 + 2 * twos:2], tallies[2:2 + 2 * twos:2]
    slack = jnp.minimum(source_of - 1, most - taker)
    passed = jax.random.randint(jax.random.fold_in(stream_key, 1), (twos,), 0, 1 << 20) % (slack + 1)
    tallies = tallies.at[1:1 + 2 * twos:2].set(source_of - passed).at[2:2 + 2 * twos:2].set(taker + passed)
    return tallies[jax.random.permutation(jax.random.fold_in(stream_key, 2), number_of)]


def scatter_about(own_key, dims, width, reach, cuts=(), kind=jnp.bfloat16):
    values = jax.random.normal(own_key, dims, jnp.float32) * width
    if len(cuts) > 0:
        values = steps_of(own_key, dims, cuts, -0.22, 0.18) * values
    return jnp.clip(values, min=-reach, max=reach).astype(kind)


def setup_inputs(seed: int = 0) -> dict:
    key_list = jax.random.split(jax.random.key(seed), 11)
    latents = draw_latents(jax.random.fold_in(key_list[10], 71), 0)
    first_gain = jnp.clip(1.0 + 0.15 * jax.random.normal(key_list[1], (C_IN,), jnp.float32), 0.25, 1.75)
    first_bias = jnp.clip(jax.random.uniform(key_list[2], (C_IN,), jnp.float32, -0.5, 0.5), -0.5, 0.5)
    first_kernel = scatter_about(key_list[3], (C_IN, 3, 3, 3, C_MID), (27 * C_IN) ** -0.5, 0.0625, ((0, 16),))
    second_gain = jnp.clip(1.0 + 0.15 * jax.random.normal(key_list[4], (C_MID,), jnp.float32), 0.25, 1.75)
    second_bias = jnp.clip(jax.random.uniform(key_list[5], (C_MID,), jnp.float32, -0.5, 0.5), -0.5, 0.5)
    second_kernel = scatter_about(key_list[6], (C_MID, 3, 3, 3, C_MID), (27 * C_MID) ** -0.5, 0.078125)
    skip_weight = scatter_about(key_list[7], (C_IN, C_MID), C_IN ** -0.5, 0.3125)
    resample_kernel = scatter_about(key_list[8], (3, 3, C_MID, C_OUT), (9 * C_MID) ** -0.5, 0.15625)
    clip_spans = uneven(key_list[9], CLIPS, SPANS, MOST_CLIP, 2).astype(jnp.int32)
    return dict(latents=latents, first_gain=first_gain, first_bias=first_bias, first_kernel=first_kernel, second_gain=second_gain, second_bias=second_bias, second_kernel=second_kernel, skip_weight=skip_weight, resample_kernel=resample_kernel, clip_spans=clip_spans)


norm_eps = 1e-06

def group_totals(volume):
    frames, height, width_cells, channels = volume.shape
    grouped = volume.astype(jnp.float32).reshape(frames, height * width_cells, GROUPS, channels // GROUPS)
    return (lax.optimization_barrier(jnp.sum(grouped, axis=(1, 3))), lax.optimization_barrier(jnp.sum(grouped * grouped, axis=(1, 3))))

def normalize(volume, totals, squares, entries, norm_gain, norm_bias):
    frames, height, width_cells, channels = volume.shape
    mean_value = totals / entries
    inv_scale = lax.rsqrt(squares / entries - mean_value * mean_value + norm_eps)
    grouped = volume.astype(jnp.float32).reshape(frames, height, width_cells, GROUPS, channels // GROUPS)
    normed = (grouped - mean_value[:, None, None, :, None]) * inv_scale[:, None, None, :, None]
    normed = normed.reshape(volume.shape) * norm_gain + norm_bias
    return jax.nn.silu(normed).astype(jnp.bfloat16)

def causal_conv(volume, kernel_all, keep_mask):
    frames = volume.shape[0]
    padded = jnp.concatenate([jnp.zeros((2,) + volume.shape[1:], jnp.float32), volume.astype(jnp.float32)], axis=0)
    running = None
    for tap_time in range(3):
        source = padded[tap_time:tap_time + frames] * keep_mask[tap_time][:, None, None, None]
        kernel = jnp.transpose(kernel_all[:, tap_time].astype(jnp.float32), (1, 2, 0, 3))
        result = lax.conv_general_dilated(source, kernel, (1, 1), ((1, 1), (1, 1)), dimension_numbers=('NHWC', 'HWIO', 'NHWC'), precision=lax.Precision.HIGHEST)
        running = result if running is None else running + result
    return running

def resample_frame(single_frame, kernel):
    enlarged = jnp.repeat(jnp.repeat(single_frame.astype(jnp.float32), 2, axis=0), 2, axis=1)
    result = lax.conv_general_dilated(enlarged[None], kernel.astype(jnp.float32), (1, 1), ((1, 1), (1, 1)), dimension_numbers=('NHWC', 'HWIO', 'NHWC'), precision=lax.Precision.HIGHEST)[0]
    return result.reshape(2 * HEIGHT, WIDTH, 2 * C_OUT).astype(jnp.bfloat16)

def reference(latents, first_gain, first_bias, first_kernel, second_gain, second_bias, second_kernel, skip_weight, resample_kernel, clip_spans):
    span_ids = (jnp.arange(FRAMES) // CF).astype(jnp.int32)
    bounds = jnp.cumsum(clip_spans).astype(jnp.int32)
    clip_of = lax.optimization_barrier(jnp.sum((span_ids[:, None] >= bounds[None, :]).astype(jnp.int32), axis=1)).astype(jnp.int32)
    earlier = jnp.concatenate([jnp.full((2,), -1, jnp.int32), clip_of])
    keep_mask = jnp.stack([(earlier[tap_time:tap_time + FRAMES] == clip_of).astype(jnp.float32) for tap_time in range(3)])
    totals, squares = group_totals(latents)
    first_act = normalize(latents, totals, squares, HEIGHT * WIDTH * (C_IN // GROUPS), first_gain, first_bias)
    hidden_first = causal_conv(first_act, first_kernel, keep_mask)
    totals, squares = group_totals(hidden_first)
    second_act = normalize(hidden_first, totals, squares, HEIGHT * WIDTH * (C_MID // GROUPS), second_gain, second_bias)
    hidden_second = causal_conv(second_act, second_kernel, keep_mask)
    shortcut = jnp.dot(latents.reshape(-1, C_IN), skip_weight, preferred_element_type=jnp.float32)
    block_out = (hidden_second + shortcut.reshape(hidden_second.shape)).astype(jnp.bfloat16)
    return lax.map(partial(resample_frame, kernel=resample_kernel), block_out)
```

```python
import functools

import jax
import jax.numpy as jnp
from jax import lax
from jax.experimental import pallas as pl
from jax.experimental.pallas import tpu as pltpu
from jax.sharding import PartitionSpec as P

GROUPS = 32
EPS = 1e-6
F32 = jnp.float32
BF16 = jnp.bfloat16
HIGHEST = lax.Precision.HIGHEST

FR, ROWS, COLS = 4, 4, 16
CIN, CMID, COUT = 384, 192, 96
SPANS, TILES = 32, 16
NX, NY, NZ = 4, 8, 8
SHARD = CIN // TILES
UNIT = 2 * SHARD
XT, YT = 12, 8
ZT = 27 - XT - YT
HEIGHT = ROWS * TILES


def member(per, transposed):
    channels = per * GROUPS
    shape = (128, channels) if transposed else (channels, 128)
    lane = lax.broadcasted_iota(jnp.int32, shape, 0 if transposed else 1)
    chan = lax.broadcasted_iota(jnp.int32, shape, 1 if transposed else 0)
    first = jnp.bitwise_and(lane, GROUPS - 1) * per
    return jnp.where((chan >= first) & (chan < first + per), 1.0, 0.0).astype(F32)


def frame_lanes(rows):
    lane = lax.broadcasted_iota(jnp.int32, (rows, 128), 1)
    row = lax.broadcasted_iota(jnp.int32, (rows, 128), 0)
    low = jnp.bitwise_and(row, FR - 1) * GROUPS
    return (lane >= low) & (lane < low + GROUPS)


def partial_stats(sums, squares, per):
    both = jnp.concatenate([sums, squares], axis=0)
    wide = jnp.dot(both, member(per, False), precision=HIGHEST, preferred_element_type=F32)
    wide = jnp.where(frame_lanes(2 * FR), wide, 0.0)
    return jnp.concatenate(
        [jnp.sum(wide[:FR], axis=0, keepdims=True), jnp.sum(wide[FR:], axis=0, keepdims=True)], axis=0
    )


def affine(total, total_prev, gain, bias, per):
    entries = float(HEIGHT * COLS * per)

    def rows_of(message):
        mean = message[0:1] / entries
        inv = lax.rsqrt(message[1:2] / entries - mean * mean + EPS)
        return [jnp.broadcast_to(mean, (FR, 128)), jnp.broadcast_to(inv, (FR, 128))]

    stacked = jnp.concatenate(rows_of(total) + rows_of(total_prev), axis=0)
    stacked = jnp.where(frame_lanes(4 * FR), stacked, 0.0)
    wide = jnp.dot(stacked, member(per, True), precision=HIGHEST, preferred_element_type=F32)
    out = []
    for at in (0, 2 * FR):
        scale = wide[at + FR : at + 2 * FR] * gain
        out.append((scale, bias - wide[at : at + FR] * scale))
    return out


def silu(v):
    half = 0.5 * v
    return half + half * jnp.tanh(half)


def shifted(a):
    zero = jnp.zeros(a.shape[:1] + (1,) + a.shape[2:], a.dtype)
    left = jnp.concatenate([zero, a[:, : COLS - 1]], axis=1)
    right = jnp.concatenate([a[:, 1:], zero], axis=1)
    return left, a, right


def kernel(
    lat, g1, b1, fk, g2, b2, sk, skw, rk, clips, out,
    xraw, fk_in, fk_pair, w1, w2, wskip, rkv, x1, hown, hraw, x2, x3, wres, acc_ref, out_v,
    mine, st_in, st_prev, mine2, st_in2, st_prev2,
    load_sem, halo_s, halo_r, stat_s, stat_r, pair_s, pair_r,
    zs, zr, xs, xr, ys, yr, ps, pr,
):
    tm = lax.axis_index("tm")
    tile = lax.axis_index("tile")
    y, x = tm // NX, lax.rem(tm, NX)
    z, core = tile // 2, lax.rem(tile, 2)
    step = 1 - 2 * core
    tm_next, tm_prev = lax.rem(tm + 1, SPANS), lax.rem(tm + SPANS - 1, SPANS)
    up, down = lax.rem(tile + TILES - 1, TILES), lax.rem(tile + 1, TILES)
    partner = (tm, tile + step)

    def along_x(by):
        return (y * NX + lax.rem(x + by + 2 * NX, NX), tile)

    def along_y(by):
        return (lax.rem(y + by + 2 * NY, NY) * NX + x, tile)

    def along_z(by):
        return (tm, lax.rem(z + by + 2 * NZ, NZ) * 2 + core)

    def remote(src, dst, send, recv, to):
        return pltpu.make_async_remote_copy(
            src_ref=src, dst_ref=dst, send_sem=send, recv_sem=recv,
            device_id=to, device_id_type=pl.DeviceIdType.MESH,
        )

    loads = [
        pltpu.make_async_copy(lat, xraw.at[2:6, 1:5], load_sem.at[0]),
        pltpu.make_async_copy(fk, fk_in, load_sem.at[1]),
        pltpu.make_async_copy(sk, w2, load_sem.at[2]),
        pltpu.make_async_copy(skw, wskip, load_sem.at[3]),
        pltpu.make_async_copy(rk, rkv, load_sem.at[4]),
    ]
    for load in loads:
        load.start()

    barrier = pltpu.get_barrier_semaphore()

    def greet(to):
        pl.semaphore_signal(barrier, inc=1, device_id=to, device_id_type=pl.DeviceIdType.MESH)

    def greet_group(i, carry):
        greet((tm, lax.rem(tile + i, TILES)))
        return carry

    def greet_prev(i, carry):
        greet((tm_prev, lax.rem(tile + i, TILES)))
        return carry

    lax.fori_loop(1, TILES, greet_group, 0)
    lax.fori_loop(0, TILES, greet_prev, 0)
    x_steps = (1, -1)
    for by in x_steps:
        greet(along_x(by))
    for by in x_steps:
        greet(along_y(by))

    loads[0].wait()
    sums, squares = [], []
    for f in range(FR):
        v = xraw[2 + f, 1:5].astype(F32).reshape(ROWS * COLS, CIN)
        sums.append(jnp.sum(v, axis=0, keepdims=True))
        squares.append(jnp.sum(v * v, axis=0, keepdims=True))
    mine[...] = partial_stats(jnp.concatenate(sums), jnp.concatenate(squares), CIN // GROUPS)
    loads[1].wait()
    pl.semaphore_wait(barrier, TILES - 1 + TILES + 4)

    def exchange(src, at_in, at_prev, phase):
        def to_group(i, carry):
            remote(
                src, at_in.at[i - 1], stat_s.at[phase, 0], stat_r.at[phase, 0],
                (tm, lax.rem(tile + i, TILES)),
            ).start()
            return carry

        def to_next(i, carry):
            remote(
                src, at_prev.at[i], stat_s.at[phase, 1], stat_r.at[phase, 1],
                (tm_next, lax.rem(tile + i, TILES)),
            ).start()
            return carry

        lax.fori_loop(1, TILES, to_group, 0)
        lax.fori_loop(0, TILES, to_next, 0)

    def exchange_wait(at_in, at_prev, phase, which):
        for i, ref in enumerate((at_in, at_prev)):
            copy = remote(ref, ref, stat_s.at[phase, i], stat_r.at[phase, i], partner)
            if which == "recv":
                copy.wait_recv()
            else:
                copy.wait_send()

    def halo_copies(ref, rim, phase):
        lo, hi = rim, rim + ROWS
        head, tail = (lo, lo + rim), (hi - rim, hi)
        cuts = [
            ((2, 6), head, (2, 6), (hi, hi + rim), (tm, up)),
            ((2, 6), tail, (2, 6), (0, rim), (tm, down)),
            ((4, 6), (lo, hi), (0, 2), (lo, hi), (tm_next, tile)),
            ((4, 6), head, (0, 2), (hi, hi + rim), (tm_next, up)),
            ((4, 6), tail, (0, 2), (0, rim), (tm_next, down)),
        ]
        return [
            remote(
                ref.at[a[0] : a[1], b[0] : b[1]], ref.at[c[0] : c[1], d[0] : d[1]],
                halo_s.at[phase, i], halo_r.at[phase, i], to,
            )
            for i, (a, b, c, d, to) in enumerate(cuts)
        ]

    pair = remote(fk_in, fk_pair, pair_s.at[0], pair_r.at[0], partner)
    pair.start()
    exchange(mine, st_in, st_prev, 0)
    halos = halo_copies(xraw, 1, 0)
    for copy in halos:
        copy.start()

    pair.wait_recv()
    odd = (core == 1).astype(F32)
    for t in range(27):
        a, b = fk_in[t].astype(F32), fk_pair[t].astype(F32)
        low, high = a + odd * (b - a), b + odd * (a - b)
        low = jnp.where(core == 1, b, a)
        high = jnp.where(core == 1, a, b)
        w1[t, z] = jnp.concatenate([low, high], axis=0).astype(BF16)

    my_x, my_y = 3 * x, XT + y
    spans = (("x", my_x, 3), ("y", my_y, 1), ("z", XT + YT, ZT))
    hops = 4

    def chip_of(k):
        return lax.rem(z - step * (k + 1) + 2 * NZ, NZ)

    def region(tap, count, chip):
        return w1.at[pl.ds(tap, count), chip]

    def z_copy(k, c):
        _, tap, count = spans[c]
        ref = region(tap, count, chip_of(k - 1))
        return remote(ref, ref, zs.at[k, c], zr.at[k, c], along_z(step))

    def x_tap(hop):
        by = (-step, -2 * step, step)[hop]
        return 3 * lax.rem(x + by + 2 * NX, NX)

    def x_copy(k, hop):
        tap = (my_x, x_tap(0), my_x)[hop]
        ref = region(tap, 3, chip_of(k))
        return remote(ref, ref, xs.at[k, hop], xr.at[k, hop], along_x((step, step, -step)[hop]))

    def y_tap(hop):
        by = -step * (hop + 1) if hop < 4 else step * (hop - 3)
        return XT + lax.rem(y + by + 2 * NY, NY)

    def y_copy(k, hop):
        tap = my_y if hop in (0, 4) else y_tap(hop - 1)
        ref = region(tap, 1, chip_of(k))
        return remote(ref, ref, ys.at[k, hop], yr.at[k, hop], along_y(step if hop < 4 else -step))

    parts = ((0, XT), (XT, YT), (XT + YT, ZT))

    def p_copy(k, c):
        ref = region(parts[c][0], parts[c][1], chip_of(k))
        return remote(ref, ref, ps.at[k, c], pr.at[k, c], partner)

    def block_guard(k, body):
        if k < hops - 1:
            body()
        else:
            pl.when(core == 0)(body)

    def z_stage(k):
        for c in (1, 0, 2):
            z_copy(k, c).wait_recv()
            if k + 1 < hops:
                block_guard(k + 1, lambda: z_copy(k + 1, c).start())
            if c == 0:
                x_copy(k, 0).start()
                x_copy(k, 2).start()
            elif c == 1:
                y_copy(k, 0).start()
                y_copy(k, 4).start()
            else:
                p_copy(k, 2).start()

    def xy_first(k):
        x_copy(k, 0).wait_recv()
        x_copy(k, 1).start()
        x_copy(k, 2).wait_recv()
        y_copy(k, 0).wait_recv()
        y_copy(k, 1).start()
        y_copy(k, 4).wait_recv()
        y_copy(k, 5).start()

    def xy_second(k):
        x_copy(k, 1).wait_recv()
        p_copy(k, 0).start()
        y_copy(k, 1).wait_recv()
        y_copy(k, 2).start()
        y_copy(k, 5).wait_recv()
        y_copy(k, 6).start()

    def y_third(k):
        y_copy(k, 2).wait_recv()
        y_copy(k, 3).start()
        y_copy(k, 6).wait_recv()

    def y_fourth(k):
        y_copy(k, 3).wait_recv()
        p_copy(k, 1).start()

    stages = (z_stage, xy_first, xy_second, y_third, y_fourth)

    def wave(s):
        for depth, stage in enumerate(stages):
            k = s - depth
            if 0 <= k < hops:
                block_guard(k, functools.partial(stage, k))

    for c in (1, 0, 2):
        z_copy(0, c).start()

    loads[4].wait()
    for a in range(2):
        for tap in range(2):
            if a == 0:
                q = [rkv[0, d].astype(F32) for d in range(3)] if tap == 0 else [
                    rkv[1, d].astype(F32) + rkv[2, d].astype(F32) for d in range(3)
                ]
            else:
                q = [rkv[0, d].astype(F32) + rkv[1, d].astype(F32) for d in range(3)] if tap == 0 else [
                    rkv[2, d].astype(F32) for d in range(3)
                ]
            none = jnp.zeros_like(q[0])
            cols = [
                jnp.concatenate([q[0], none], axis=1),
                jnp.concatenate([q[1] + q[2], q[0] + q[1]], axis=1),
                jnp.concatenate([none, q[2]], axis=1),
            ]
            for d in range(3):
                wres[a, (tap * 3 + d) * CMID : (tap * 3 + d + 1) * CMID, :] = cols[d].astype(BF16)

    total = clips[0] * 0
    starts_here = span_start(clips, tm)
    keep_prev = jnp.where(starts_here, 0.0, 1.0).astype(F32)
    keep_top = jnp.where(tile == 0, 0.0, 1.0).astype(F32)
    keep_bottom = jnp.where(tile == TILES - 1, 0.0, 1.0).astype(F32)

    exchange_wait(st_in, st_prev, 0, "recv")
    total = jnp.sum(st_in[...], axis=0) + mine[...]
    total_prev = jnp.sum(st_prev[...], axis=0)
    own, prev = affine(total, total_prev, g1[...], b1[...], CIN // GROUPS)
    for copy in halos:
        copy.wait_recv()
    for f in range(6):
        scale, shift = (own[0][f - 2], own[1][f - 2]) if f >= 2 else (prev[0][f + 2], prev[1][f + 2])
        v = xraw[f].astype(F32) * scale[None, None, :] + shift[None, None, :]
        a = silu(v)
        if f < 2:
            a = a * keep_prev
        a = jnp.concatenate([a[0:1] * keep_top, a[1:5], a[5:6] * keep_bottom], axis=0)
        for d, part in enumerate(shifted(a)):
            x1[f, :, :, d * CIN : (d + 1) * CIN] = part.astype(BF16)

    for s in range(hops + len(stages) - 1):
        wave(s)

    def partner_wait(c):
        for k in range(hops):
            ref = region(parts[c][0], parts[c][1], 0)
            copy = remote(ref, ref, ps.at[k, c], pr.at[k, c], partner)
            if k < hops - 1:
                copy.wait_recv()
            else:
                pl.when(core == 1)(copy.wait_recv)

    def conv1(groups, first):
        total = None if first else acc_ref[...]
        for g in groups:
            s, dy = divmod(g, 3)
            window = x1[s : s + FR, dy : dy + ROWS].reshape(FR * ROWS * COLS, 3 * CIN)
            weights = w1[3 * g : 3 * g + 3].reshape(3 * CIN, CMID)
            term = jnp.dot(window, weights, preferred_element_type=F32)
            total = term if total is None else total + term
        acc_ref[...] = total

    partner_wait(2)
    conv1((7, 8), True)
    partner_wait(0)
    conv1((0, 1, 2, 3), False)
    partner_wait(1)
    conv1((4, 5, 6), False)

    hidden = acc_ref[...].reshape(FR, ROWS * COLS, CMID)
    hown[...] = hidden.reshape(FR, ROWS, COLS, CMID)
    hraw[2:6, 2:6] = hidden.reshape(FR, ROWS, COLS, CMID).astype(BF16)
    halos2 = halo_copies(hraw, 2, 1)
    for copy in halos2:
        copy.start()
    mine2[...] = partial_stats(jnp.sum(hidden, axis=1), jnp.sum(hidden * hidden, axis=1), CMID // GROUPS)
    exchange(mine2, st_in2, st_prev2, 1)

    loads[3].wait()
    loads[2].wait()
    shortcut = lax.dot_general(
        xraw[2:6].reshape(FR * 6 * COLS, CIN), wskip[...], (((1,), (1,)), ((), ())),
        preferred_element_type=F32,
    )

    exchange_wait(st_in2, st_prev2, 1, "recv")
    total = jnp.sum(st_in2[...], axis=0) + mine2[...]
    total_prev = jnp.sum(st_prev2[...], axis=0)
    own, prev = affine(total, total_prev, g2[...], b2[...], CMID // GROUPS)
    for copy in halos2:
        copy.wait_recv()
    for f in range(6):
        scale, shift = (own[0][f - 2], own[1][f - 2]) if f >= 2 else (prev[0][f + 2], prev[1][f + 2])
        if f >= 2:
            v = jnp.concatenate(
                [hraw[f, 0:2].astype(F32), hown[f - 2], hraw[f, 6:8].astype(F32)], axis=0
            )
        else:
            v = hraw[f].astype(F32)
        a = silu(v * scale[None, None, :] + shift[None, None, :])
        if f < 2:
            a = a * keep_prev
        a = jnp.concatenate([a[0:2] * keep_top, a[2:6], a[6:8] * keep_bottom], axis=0)
        x2[f] = jnp.concatenate(shifted(a), axis=-1).astype(BF16)

    total = shortcut
    for g in range(9):
        s, dy = divmod(g, 3)
        window = x2[s : s + FR, dy : dy + 6].reshape(FR * 6 * COLS, 3 * CMID)
        weights = w2[3 * g : 3 * g + 3].reshape(3 * CMID, CMID)
        total = total + jnp.dot(window, weights, preferred_element_type=F32)
    block = total.astype(BF16).astype(F32).reshape(FR, 6, COLS, CMID)
    for f in range(FR):
        a = jnp.concatenate(
            [block[f, 0:1] * keep_top, block[f, 1:5], block[f, 5:6] * keep_bottom], axis=0
        )
        x3[f] = jnp.concatenate(shifted(a), axis=-1).astype(BF16)

    for a in range(2):
        window = jnp.concatenate(
            [x3[:, a : a + ROWS], x3[:, a + 1 : a + 1 + ROWS]], axis=-1
        ).reshape(FR * ROWS * COLS, 6 * CMID)
        res = jnp.dot(window, wres[a], preferred_element_type=F32)
        res = res.astype(BF16).reshape(FR, ROWS, COLS, 2 * COUT)
        out_v[:, :, a] = res
    store = pltpu.make_async_copy(out_v, out, load_sem.at[5])
    store.start()

    pair.wait_send()
    for copy in halos + halos2:
        copy.wait_send()
    exchange_wait(st_in, st_prev, 0, "send")
    exchange_wait(st_in2, st_prev2, 1, "send")

    def drain(k):
        for c in range(3):
            z_copy(k, c).wait_send()
            p_copy(k, c).wait_send()
            x_copy(k, c).wait_send()
        for hop in range(7):
            y_copy(k, hop).wait_send()

    for k in range(hops):
        block_guard(k, functools.partial(drain, k))
    store.wait()


def span_start(clips, tm):
    start, hit = jnp.int32(0), tm == 0
    for j in range(3):
        start = start + clips[j]
        hit = hit | (start == tm)
    return hit


def shards(
    latents, first_gain, first_bias, first_kernel, second_gain, second_bias,
    second_kernel, skip_weight, resample_kernel, clip_spans,
):
    fk = jnp.transpose(first_kernel, (1, 2, 3, 0, 4)).reshape(27, SHARD, CMID)
    sk = jnp.transpose(second_kernel, (1, 2, 3, 0, 4)).reshape(27, CMID, CMID)
    anywhere = pl.BlockSpec(memory_space=pl.ANY)
    vmem = pl.BlockSpec(memory_space=pltpu.VMEM)
    smem = pl.BlockSpec(memory_space=pltpu.SMEM)
    dma = pltpu.SemaphoreType.DMA
    out = pl.pallas_call(
        kernel,
        out_shape=jax.ShapeDtypeStruct((FR, ROWS, 2, COLS, 2 * COUT), BF16),
        in_specs=[anywhere, vmem, vmem, anywhere, vmem, vmem, anywhere, anywhere, anywhere, smem],
        out_specs=anywhere,
        scratch_shapes=[
            pltpu.VMEM((6, 6, COLS, CIN), BF16),
            pltpu.VMEM((27, SHARD, CMID), BF16),
            pltpu.VMEM((27, SHARD, CMID), BF16),
            pltpu.VMEM((27, NZ, UNIT, CMID), BF16),
            pltpu.VMEM((27, CMID, CMID), BF16),
            pltpu.VMEM((CMID, CIN), BF16),
            pltpu.VMEM((3, 3, CMID, COUT), BF16),
            pltpu.VMEM((6, 6, COLS, 3 * CIN), BF16),
            pltpu.VMEM((FR, ROWS, COLS, CMID), F32),
            pltpu.VMEM((6, 8, COLS, CMID), BF16),
            pltpu.VMEM((6, 8, COLS, 3 * CMID), BF16),
            pltpu.VMEM((FR, 6, COLS, 3 * CMID), BF16),
            pltpu.VMEM((2, 6 * CMID, 2 * COUT), BF16),
            pltpu.VMEM((FR * ROWS * COLS, CMID), F32),
            pltpu.VMEM((FR, ROWS, 2, COLS, 2 * COUT), BF16),
            pltpu.VMEM((2, 128), F32),
            pltpu.VMEM((TILES - 1, 2, 128), F32),
            pltpu.VMEM((TILES, 2, 128), F32),
            pltpu.VMEM((2, 128), F32),
            pltpu.VMEM((TILES - 1, 2, 128), F32),
            pltpu.VMEM((TILES, 2, 128), F32),
            dma((6,)),
            dma((2, 5)), dma((2, 5)),
            dma((2, 2)), dma((2, 2)),
            dma((1,)), dma((1,)),
            dma((4, 3)), dma((4, 3)),
            dma((4, 3)), dma((4, 3)),
            dma((4, 7)), dma((4, 7)),
            dma((4, 3)), dma((4, 3)),
        ],
        compiler_params=pltpu.CompilerParams(
            collective_id=0, has_side_effects=True, vmem_limit_bytes=56 * 2**20
        ),
    )(
        latents, first_gain.reshape(1, CIN), first_bias.reshape(1, CIN), fk,
        second_gain.reshape(1, CMID), second_bias.reshape(1, CMID), sk, skip_weight.T,
        resample_kernel, clip_spans,
    )
    return out.reshape(FR, 2 * ROWS, COLS, 2 * COUT)


def solution(mesh):
    in_specs = (
        P("tm", "tile", None, None), P(), P(), P("tile", None, None, None, None),
        P(), P(), P(), P(), P(), P(),
    )
    return jax.shard_map(
        shards, mesh=mesh, in_specs=in_specs, out_specs=P("tm", "tile", None, None), check_vma=False
    )
```

```python
import functools

import jax
import jax.numpy as jnp
from jax import lax
from jax.experimental import pallas as pl
from jax.experimental.pallas import tpu as pltpu
from jax.sharding import PartitionSpec as P

GROUPS = 32
EPS = 1e-6
F32 = jnp.float32
BF16 = jnp.bfloat16
HIGHEST = lax.Precision.HIGHEST

FR, ROWS, COLS = 4, 4, 16
CIN, CMID, COUT = 384, 192, 96
SPANS, TILES = 32, 16
NX, NY, NZ = 4, 8, 8
SHARD = CIN // TILES
UNIT = 2 * SHARD
UNITS = 41
XU, YU = 6, 2
XT, YT = XU * NX, YU * NY
ZT = UNITS - XT - YT
HEIGHT = ROWS * TILES


def member(per, transposed):
    channels = per * GROUPS
    shape = (128, channels) if transposed else (channels, 128)
    lane = lax.broadcasted_iota(jnp.int32, shape, 0 if transposed else 1)
    chan = lax.broadcasted_iota(jnp.int32, shape, 1 if transposed else 0)
    first = jnp.bitwise_and(lane, GROUPS - 1) * per
    return jnp.where((chan >= first) & (chan < first + per), 1.0, 0.0).astype(F32)


def frame_lanes(rows):
    lane = lax.broadcasted_iota(jnp.int32, (rows, 128), 1)
    row = lax.broadcasted_iota(jnp.int32, (rows, 128), 0)
    low = jnp.bitwise_and(row, FR - 1) * GROUPS
    return (lane >= low) & (lane < low + GROUPS)


def partial_stats(sums, squares, per):
    both = jnp.concatenate([sums, squares], axis=0)
    wide = jnp.dot(both, member(per, False), precision=HIGHEST, preferred_element_type=F32)
    wide = jnp.where(frame_lanes(2 * FR), wide, 0.0)
    return jnp.concatenate(
        [jnp.sum(wide[:FR], axis=0, keepdims=True), jnp.sum(wide[FR:], axis=0, keepdims=True)], axis=0
    )


def affine(total, total_prev, gain, bias, per):
    entries = float(HEIGHT * COLS * per)

    def rows_of(message):
        mean = message[0:1] / entries
        inv = lax.rsqrt(message[1:2] / entries - mean * mean + EPS)
        return [jnp.broadcast_to(mean, (FR, 128)), jnp.broadcast_to(inv, (FR, 128))]

    stacked = jnp.concatenate(rows_of(total) + rows_of(total_prev), axis=0)
    stacked = jnp.where(frame_lanes(4 * FR), stacked, 0.0)
    wide = jnp.dot(stacked, member(per, True), precision=HIGHEST, preferred_element_type=F32)
    out = []
    for at in (0, 2 * FR):
        scale = wide[at + FR : at + 2 * FR] * gain
        out.append((scale, bias - wide[at : at + FR] * scale))
    return out


def silu(v):
    half = 0.5 * v
    return half + half * jnp.tanh(half)


def shifted(a):
    zero = jnp.zeros(a.shape[:1] + (1,) + a.shape[2:], a.dtype)
    left = jnp.concatenate([zero, a[:, : COLS - 1]], axis=1)
    right = jnp.concatenate([a[:, 1:], zero], axis=1)
    return left, a, right


def kernel(
    lat, g1, b1, fk, g2, b2, sk, skw, rk, clips, out,
    xraw, fk_in, fk_pair, w1, w2, wskip, rkv, x1, hown, hraw, x2, x3, wres, acc_ref, out_v,
    mine, st_in, st_total, st_prev, mine2, st_in2, st_total2, st_prev2,
    load_sem, halo_s, halo_r, stat_s, stat_r, pair_s, pair_r,
    zs, zr, xs, xr, ys, yr, ps, pr,
):
    tm = lax.axis_index("tm")
    tile = lax.axis_index("tile")
    y, x = tm // NX, lax.rem(tm, NX)
    z, core = tile // 2, lax.rem(tile, 2)
    step = 1 - 2 * core
    tm_next, tm_prev = lax.rem(tm + 1, SPANS), lax.rem(tm + SPANS - 1, SPANS)
    up, down = lax.rem(tile + TILES - 1, TILES), lax.rem(tile + 1, TILES)
    partner = (tm, tile + step)

    def along_x(by):
        return (y * NX + lax.rem(x + by + 2 * NX, NX), tile)

    def along_y(by):
        return (lax.rem(y + by + 2 * NY, NY) * NX + x, tile)

    def along_z(by):
        return (tm, lax.rem(z + by + 2 * NZ, NZ) * 2 + core)

    def remote(src, dst, send, recv, to):
        return pltpu.make_async_remote_copy(
            src_ref=src, dst_ref=dst, send_sem=send, recv_sem=recv,
            device_id=to, device_id_type=pl.DeviceIdType.MESH,
        )

    loads = [
        pltpu.make_async_copy(lat, xraw.at[2:6, 1:5], load_sem.at[0]),
        pltpu.make_async_copy(fk, fk_in, load_sem.at[1]),
        pltpu.make_async_copy(sk, w2, load_sem.at[2]),
        pltpu.make_async_copy(skw, wskip, load_sem.at[3]),
        pltpu.make_async_copy(rk, rkv, load_sem.at[4]),
    ]
    for load in loads:
        load.start()

    barrier = pltpu.get_barrier_semaphore()
    near = [along_x(1), along_x(-1), along_y(1), along_y(-1), along_y(2), along_y(-2)]
    near += [(tm_prev, tile), (tm_prev, up), (tm_prev, down)]

    def greet(to):
        pl.semaphore_signal(barrier, inc=1, device_id=to, device_id_type=pl.DeviceIdType.MESH)

    def greet_group(i, carry):
        greet((tm, lax.rem(tile + i, TILES)))
        return carry

    lax.fori_loop(1, TILES, greet_group, 0)
    for to in near:
        greet(to)

    loads[0].wait()
    sums, squares = [], []
    for f in range(FR):
        v = xraw[2 + f, 1:5].astype(F32).reshape(ROWS * COLS, CIN)
        sums.append(jnp.sum(v, axis=0, keepdims=True))
        squares.append(jnp.sum(v * v, axis=0, keepdims=True))
    mine[...] = partial_stats(jnp.concatenate(sums), jnp.concatenate(squares), CIN // GROUPS)
    loads[1].wait()
    pl.semaphore_wait(barrier, TILES - 1 + len(near))

    def exchange(src, at_in, phase):
        def to_group(i, carry):
            remote(
                src, at_in.at[i - 1], stat_s.at[phase, 0], stat_r.at[phase, 0],
                (tm, lax.rem(tile + i, TILES)),
            ).start()
            return carry

        lax.fori_loop(1, TILES, to_group, 0)

    def exchange_copy(at_in, phase):
        return remote(at_in, at_in, stat_s.at[phase, 0], stat_r.at[phase, 0], partner)

    def relay(total, at_prev, phase):
        return remote(total, at_prev, stat_s.at[phase, 1], stat_r.at[phase, 1], (tm_next, tile))

    def halo_copies(ref, rim, phase):
        lo, hi = rim, rim + ROWS
        head, tail = (lo, lo + rim), (hi - rim, hi)
        cuts = [
            ((2, 6), head, (2, 6), (hi, hi + rim), (tm, up)),
            ((2, 6), tail, (2, 6), (0, rim), (tm, down)),
            ((4, 6), (lo, hi), (0, 2), (lo, hi), (tm_next, tile)),
            ((4, 6), head, (0, 2), (hi, hi + rim), (tm_next, up)),
            ((4, 6), tail, (0, 2), (0, rim), (tm_next, down)),
        ]
        return [
            remote(
                ref.at[a[0] : a[1], b[0] : b[1]], ref.at[c[0] : c[1], d[0] : d[1]],
                halo_s.at[phase, i], halo_r.at[phase, i], to,
            )
            for i, (a, b, c, d, to) in enumerate(cuts)
        ]

    pair = remote(fk_in, fk_pair, pair_s.at[0], pair_r.at[0], partner)
    pair.start()
    exchange(mine, st_in, 0)
    halos = halo_copies(xraw, 1, 0)
    for copy in halos:
        copy.start()

    pair.wait_recv()

    def both_halves(t):
        a, b = fk_in[t].astype(F32), fk_pair[t].astype(F32)
        return jnp.concatenate([jnp.where(core == 1, b, a), jnp.where(core == 1, a, b)], axis=0)

    for p in range(14):
        even = both_halves(2 * p)
        w1[3 * p, z] = even[:, :128].astype(BF16)
        if p < 13:
            odd = both_halves(2 * p + 1)
            w1[3 * p + 1, z] = odd[:, :128].astype(BF16)
            rest = jnp.concatenate([even[:, 128:], odd[:, 128:]], axis=1)
            w1[3 * p + 2, z] = rest.astype(BF16)
        else:
            rest = jnp.concatenate([even[:, 128:], jnp.zeros_like(even[:, 128:])], axis=1)
            w1[3 * p + 1, z] = rest.astype(BF16)

    my_x, my_y = XU * x, XT + YU * y
    spans = ((my_x, XU), (my_y, YU), (XT + YT, ZT))
    hops = 4

    def chip_of(k):
        return lax.rem(z - step * (k + 1) + 2 * NZ, NZ)

    def region(unit, count, chip):
        return w1.at[pl.ds(unit, count), chip]

    def z_copy(k, c):
        unit, count = spans[c]
        if c == 1 or k < 2:
            ref, by = region(unit, count, z), step * (k + 1)
        else:
            ref, by = region(unit, count, chip_of(1)), step * (k - 1)
        return remote(ref, ref, zs.at[k, c], zr.at[k, c], along_z(by))

    def x_copy(k, hop):
        unit = my_x if hop != 1 else XU * lax.rem(x - step + NX, NX)
        ref = region(unit, XU, chip_of(k))
        return remote(ref, ref, xs.at[k, hop], xr.at[k, hop], along_x((step, step, -step)[hop]))

    def y_copy(k, hop):
        origin = {2: -2 * step, 3: -2 * step, 6: 2 * step}.get(hop, 0)
        by = (step, 2 * step, step, 2 * step, -step, -2 * step, -step)[hop]
        unit = XT + YU * lax.rem(y + origin + NY, NY)
        ref = region(unit, YU, chip_of(k))
        return remote(ref, ref, ys.at[k, hop], yr.at[k, hop], along_y(by))

    parts = ((0, XT), (XT, YT), (XT + YT, ZT))

    def p_copy(k, c):
        ref = region(parts[c][0], parts[c][1], chip_of(k))
        return remote(ref, ref, ps.at[k, c], pr.at[k, c], partner)

    def block_guard(k, body):
        if k < hops - 1:
            body()
        else:
            pl.when(core == 0)(body)

    def z_start():
        for k in (3, 2, 1, 0):
            block_guard(k, lambda: z_copy(k, 1).start())
        for k in (0, 1):
            z_copy(k, 0).start()
        for k in (0, 1):
            z_copy(k, 2).start()

    def zy_arrived(k):
        z_copy(k, 1).wait_recv()
        for hop in (1, 5, 0, 4):
            y_copy(k, hop).start()

    def zx_arrived(k):
        z_copy(k, 0).wait_recv()
        if k == 1:
            z_copy(2, 0).start()
            block_guard(3, lambda: z_copy(3, 0).start())
        x_copy(k, 0).start()
        x_copy(k, 2).start()

    def zz_arrived(k):
        z_copy(k, 2).wait_recv()
        if k == 1:
            z_copy(2, 2).start()
            block_guard(3, lambda: z_copy(3, 2).start())
        p_copy(k, 2).start()

    def y_near(k):
        y_copy(k, 1).wait_recv()
        y_copy(k, 3).start()
        y_copy(k, 2).start()
        y_copy(k, 5).wait_recv()
        y_copy(k, 6).start()

    def y_rest(k):
        for hop in (0, 4, 2, 6, 3):
            y_copy(k, hop).wait_recv()
        p_copy(k, 1).start()

    def x_near(k):
        x_copy(k, 0).wait_recv()
        x_copy(k, 1).start()

    def x_rest(k):
        x_copy(k, 2).wait_recv()
        x_copy(k, 1).wait_recv()
        p_copy(k, 0).start()

    def run(stage, *blocks):
        for k in blocks:
            block_guard(k, functools.partial(stage, k))

    z_start()

    loads[4].wait()
    for a in range(2):
        for tap in range(2):
            if a == 0:
                q = [rkv[0, d].astype(F32) for d in range(3)] if tap == 0 else [
                    rkv[1, d].astype(F32) + rkv[2, d].astype(F32) for d in range(3)
                ]
            else:
                q = [rkv[0, d].astype(F32) + rkv[1, d].astype(F32) for d in range(3)] if tap == 0 else [
                    rkv[2, d].astype(F32) for d in range(3)
                ]
            none = jnp.zeros_like(q[0])
            cols = [
                jnp.concatenate([q[0], none], axis=1),
                jnp.concatenate([q[1] + q[2], q[0] + q[1]], axis=1),
                jnp.concatenate([none, q[2]], axis=1),
            ]
            for d in range(3):
                wres[a, (tap * 3 + d) * CMID : (tap * 3 + d + 1) * CMID, :] = cols[d].astype(BF16)

    starts_here = span_start(clips, tm)
    keep_prev = jnp.where(starts_here, 0.0, 1.0).astype(F32)
    keep_top = jnp.where(tile == 0, 0.0, 1.0).astype(F32)
    keep_bottom = jnp.where(tile == TILES - 1, 0.0, 1.0).astype(F32)

    exchange_copy(st_in, 0).wait_recv()
    st_total[...] = jnp.sum(st_in[...], axis=0) + mine[...]
    relayed = relay(st_total, st_prev, 0)
    relayed.start()
    run(zy_arrived, 0, 1, 2, 3)
    run(zx_arrived, 0, 1)
    relayed.wait_recv()
    own, prev = affine(
        st_total[...], st_prev[...], g1[...].reshape(1, CIN), b1[...].reshape(1, CIN), CIN // GROUPS
    )
    for copy in halos:
        copy.wait_recv()
    for f in range(6):
        scale, shift = (own[0][f - 2], own[1][f - 2]) if f >= 2 else (prev[0][f + 2], prev[1][f + 2])
        v = xraw[f].astype(F32) * scale[None, None, :] + shift[None, None, :]
        a = silu(v)
        if f < 2:
            a = a * keep_prev
        a = jnp.concatenate([a[0:1] * keep_top, a[1:5], a[5:6] * keep_bottom], axis=0)
        for d, part in enumerate(shifted(a)):
            x1[f, :, :, d * CIN : (d + 1) * CIN] = part.astype(BF16)

    run(y_near, 0, 1, 2, 3)
    run(x_near, 0, 1)
    run(zx_arrived, 2, 3)
    run(zz_arrived, 0, 1, 2, 3)
    run(x_rest, 0, 1)
    run(y_rest, 0, 1, 2, 3)
    run(x_near, 2, 3)
    run(x_rest, 2, 3)

    def partner_wait(c):
        for k in range(hops):
            ref = region(parts[c][0], parts[c][1], 0)
            copy = remote(ref, ref, ps.at[k, c], pr.at[k, c], partner)
            if k < hops - 1:
                copy.wait_recv()
            else:
                pl.when(core == 1)(copy.wait_recv)

    def tap_window(t):
        s, rest = divmod(t, 9)
        dy, dx = divmod(rest, 3)
        window = x1[s : s + FR, dy : dy + ROWS, :, dx * CIN : (dx + 1) * CIN]
        return window.reshape(FR * ROWS * COLS, CIN)

    def conv1(pairs, first):
        total = [None, None] if first else [acc_ref[0], acc_ref[1]]
        for p in pairs:
            rest = w1[3 * p + (2 if p < 13 else 1)].reshape(CIN, 128)
            for odd in range(2 if p < 13 else 1):
                weights = jnp.concatenate([w1[3 * p + odd].reshape(CIN, 128), rest], axis=1)
                term = jnp.dot(tap_window(2 * p + odd), weights, preferred_element_type=F32)
                total[odd] = term if total[odd] is None else total[odd] + term
        acc_ref[0], acc_ref[1] = total

    partner_wait(1)
    partner_wait(2)
    conv1(range(8, 14), True)
    partner_wait(0)
    conv1(range(0, 8), False)

    even, odd = acc_ref[0], acc_ref[1]
    hidden = jnp.concatenate([even[:, :128] + odd[:, :128], even[:, 128:192] + odd[:, 192:]], axis=1)
    hidden = hidden.reshape(FR, ROWS * COLS, CMID)
    hown[...] = hidden.reshape(FR, ROWS, COLS, CMID)
    hraw[2:6, 2:6] = hidden.reshape(FR, ROWS, COLS, CMID).astype(BF16)
    halos2 = halo_copies(hraw, 2, 1)
    for copy in halos2:
        copy.start()
    mine2[...] = partial_stats(jnp.sum(hidden, axis=1), jnp.sum(hidden * hidden, axis=1), CMID // GROUPS)
    exchange(mine2, st_in2, 1)

    loads[3].wait()
    loads[2].wait()
    shortcut = lax.dot_general(
        xraw[2:6].reshape(FR * 6 * COLS, CIN), wskip[...], (((1,), (1,)), ((), ())),
        preferred_element_type=F32,
    )

    exchange_copy(st_in2, 1).wait_recv()
    st_total2[...] = jnp.sum(st_in2[...], axis=0) + mine2[...]
    relayed2 = relay(st_total2, st_prev2, 1)
    relayed2.start()
    relayed2.wait_recv()
    own, prev = affine(
        st_total2[...], st_prev2[...], g2[...].reshape(1, CMID), b2[...].reshape(1, CMID), CMID // GROUPS
    )
    for copy in halos2:
        copy.wait_recv()
    for f in range(6):
        scale, shift = (own[0][f - 2], own[1][f - 2]) if f >= 2 else (prev[0][f + 2], prev[1][f + 2])
        if f >= 2:
            v = jnp.concatenate(
                [hraw[f, 0:2].astype(F32), hown[f - 2], hraw[f, 6:8].astype(F32)], axis=0
            )
        else:
            v = hraw[f].astype(F32)
        a = silu(v * scale[None, None, :] + shift[None, None, :])
        if f < 2:
            a = a * keep_prev
        a = jnp.concatenate([a[0:2] * keep_top, a[2:6], a[6:8] * keep_bottom], axis=0)
        x2[f] = jnp.concatenate(shifted(a), axis=-1).astype(BF16)

    total = shortcut
    for g in range(9):
        s, dy = divmod(g, 3)
        window = x2[s : s + FR, dy : dy + 6].reshape(FR * 6 * COLS, 3 * CMID)
        weights = w2[3 * g : 3 * g + 3].reshape(3 * CMID, CMID)
        total = total + jnp.dot(window, weights, preferred_element_type=F32)
    block = total.astype(BF16).astype(F32).reshape(FR, 6, COLS, CMID)
    for f in range(FR):
        a = jnp.concatenate(
            [block[f, 0:1] * keep_top, block[f, 1:5], block[f, 5:6] * keep_bottom], axis=0
        )
        x3[f] = jnp.concatenate(shifted(a), axis=-1).astype(BF16)

    for a in range(2):
        window = jnp.concatenate(
            [x3[:, a : a + ROWS], x3[:, a + 1 : a + 1 + ROWS]], axis=-1
        ).reshape(FR * ROWS * COLS, 6 * CMID)
        res = jnp.dot(window, wres[a], preferred_element_type=F32)
        res = res.astype(BF16).reshape(FR, ROWS, COLS, 2 * COUT)
        out_v[:, :, a] = res
    store = pltpu.make_async_copy(out_v, out, load_sem.at[5])
    store.start()

    pair.wait_send()
    for copy in halos + halos2:
        copy.wait_send()
    for copy in (exchange_copy(st_in, 0), exchange_copy(st_in2, 1), relayed, relayed2):
        copy.wait_send()

    def drain(k):
        for c in range(3):
            z_copy(k, c).wait_send()
            p_copy(k, c).wait_send()
            x_copy(k, c).wait_send()
        for hop in range(7):
            y_copy(k, hop).wait_send()

    for k in range(hops):
        block_guard(k, functools.partial(drain, k))
    store.wait()


def span_start(clips, tm):
    start, hit = jnp.int32(0), tm == 0
    for j in range(3):
        start = start + clips[j]
        hit = hit | (start == tm)
    return hit


def shards(
    latents, first_gain, first_bias, first_kernel, second_gain, second_bias,
    second_kernel, skip_weight, resample_kernel, clip_spans,
):
    fk = jnp.transpose(first_kernel, (1, 2, 3, 0, 4)).reshape(27, SHARD, CMID)
    sk = jnp.transpose(second_kernel, (1, 2, 3, 0, 4)).reshape(27, CMID, CMID)
    anywhere = pl.BlockSpec(memory_space=pl.ANY)
    vmem = pl.BlockSpec(memory_space=pltpu.VMEM)
    smem = pl.BlockSpec(memory_space=pltpu.SMEM)
    dma = pltpu.SemaphoreType.DMA
    out = pl.pallas_call(
        kernel,
        out_shape=jax.ShapeDtypeStruct((FR, ROWS, 2, COLS, 2 * COUT), BF16),
        in_specs=[anywhere, vmem, vmem, anywhere, vmem, vmem, anywhere, anywhere, anywhere, smem],
        out_specs=anywhere,
        scratch_shapes=[
            pltpu.VMEM((6, 6, COLS, CIN), BF16),
            pltpu.VMEM((27, SHARD, CMID), BF16),
            pltpu.VMEM((27, SHARD, CMID), BF16),
            pltpu.VMEM((UNITS, NZ, UNIT, 128), BF16),
            pltpu.VMEM((27, CMID, CMID), BF16),
            pltpu.VMEM((CMID, CIN), BF16),
            pltpu.VMEM((3, 3, CMID, COUT), BF16),
            pltpu.VMEM((6, 6, COLS, 3 * CIN), BF16),
            pltpu.VMEM((FR, ROWS, COLS, CMID), F32),
            pltpu.VMEM((6, 8, COLS, CMID), BF16),
            pltpu.VMEM((6, 8, COLS, 3 * CMID), BF16),
            pltpu.VMEM((FR, 6, COLS, 3 * CMID), BF16),
            pltpu.VMEM((2, 6 * CMID, 2 * COUT), BF16),
            pltpu.VMEM((2, FR * ROWS * COLS, 256), F32),
            pltpu.VMEM((FR, ROWS, 2, COLS, 2 * COUT), BF16),
            pltpu.VMEM((2, 128), F32),
            pltpu.VMEM((TILES - 1, 2, 128), F32),
            pltpu.VMEM((2, 128), F32),
            pltpu.VMEM((2, 128), F32),
            pltpu.VMEM((2, 128), F32),
            pltpu.VMEM((TILES - 1, 2, 128), F32),
            pltpu.VMEM((2, 128), F32),
            pltpu.VMEM((2, 128), F32),
            dma((6,)),
            dma((2, 5)), dma((2, 5)),
            dma((2, 2)), dma((2, 2)),
            dma((1,)), dma((1,)),
            dma((4, 3)), dma((4, 3)),
            dma((4, 3)), dma((4, 3)),
            dma((4, 7)), dma((4, 7)),
            dma((4, 3)), dma((4, 3)),
        ],
        compiler_params=pltpu.CompilerParams(
            collective_id=0, has_side_effects=True, vmem_limit_bytes=56 * 2**20
        ),
    )(
        latents, first_gain, first_bias, fk,
        second_gain, second_bias, sk, skip_weight.T,
        resample_kernel, clip_spans,
    )
    return out.reshape(FR, 2 * ROWS, COLS, 2 * COUT)


def solution(mesh):
    in_specs = (
        P("tm", "tile", None, None), P(), P(), P("tile", None, None, None, None),
        P(), P(), P(), P(), P(), P(),
    )
    return jax.shard_map(
        shards, mesh=mesh, in_specs=in_specs, out_specs=P("tm", "tile", None, None), check_vma=False
    )
```

```python
import functools

import jax
import jax.numpy as jnp
from jax import lax
from jax.experimental import pallas as pl
from jax.experimental.pallas import tpu as pltpu
from jax.sharding import PartitionSpec as P

GROUPS = 32
EPS = 1e-6
F32 = jnp.float32
BF16 = jnp.bfloat16

FR, ROWS, COLS = 4, 4, 16
CIN, CMID, COUT = 384, 192, 96
SPANS, TILES = 32, 16
NX, NY, NZ = 4, 8, 8
SHARD = CIN // TILES
UNIT = 2 * SHARD
UNITS = 41
XU = 8
XT = XU * NX
ZT = UNITS - XT
HEIGHT = ROWS * TILES


def member(per, transposed):
    channels = per * GROUPS
    shape = (128, channels) if transposed else (channels, 128)
    lane = lax.broadcasted_iota(jnp.int32, shape, 0 if transposed else 1)
    chan = lax.broadcasted_iota(jnp.int32, shape, 1 if transposed else 0)
    first = jnp.bitwise_and(lane, GROUPS - 1) * per
    return jnp.where((chan >= first) & (chan < first + per), 1.0, 0.0).astype(BF16)


def frame_lanes(rows):
    lane = lax.broadcasted_iota(jnp.int32, (rows, 128), 1)
    row = lax.broadcasted_iota(jnp.int32, (rows, 128), 0)
    low = jnp.bitwise_and(row, FR - 1) * GROUPS
    return (lane >= low) & (lane < low + GROUPS)


def exact_dot(values, zero_one):
    rows = values.shape[0]
    high = values.astype(BF16).astype(F32)
    left = values - high
    middle = left.astype(BF16).astype(F32)
    terms = jnp.concatenate([high, middle, left - middle], axis=0).astype(BF16)
    wide = jnp.dot(terms, zero_one, preferred_element_type=F32)
    return wide[:rows] + wide[rows : 2 * rows] + wide[2 * rows :]


def partial_stats(sums, squares, to_lanes):
    wide = exact_dot(jnp.concatenate([sums, squares], axis=0), to_lanes)
    wide = jnp.where(frame_lanes(2 * FR), wide, 0.0)
    return jnp.concatenate(
        [jnp.sum(wide[:FR], axis=0, keepdims=True), jnp.sum(wide[FR:], axis=0, keepdims=True)], axis=0
    )


def affine(message, gain, bias, per, to_channels):
    entries = float(HEIGHT * COLS * per)
    mean = message[0:1] / entries
    inv = lax.rsqrt(message[1:2] / entries - mean * mean + EPS)
    stacked = jnp.concatenate([jnp.broadcast_to(mean, (FR, 128)), jnp.broadcast_to(inv, (FR, 128))], axis=0)
    wide = exact_dot(jnp.where(frame_lanes(2 * FR), stacked, 0.0), to_channels)
    scale = wide[FR:] * gain
    return scale, bias - wide[:FR] * scale


def silu(v):
    half = 0.5 * v
    return half + half * jnp.tanh(half)


def shifted(a):
    zero = jnp.zeros(a.shape[:1] + (1,) + a.shape[2:], a.dtype)
    left = jnp.concatenate([zero, a[:, : COLS - 1]], axis=1)
    right = jnp.concatenate([a[:, 1:], zero], axis=1)
    return left, a, right


def kernel(
    lat, g1, b1, fk, g2, b2, sk, skw, rk, clips, out,
    xraw, fk_in, fk_pair, w1, w2, wskip, rkv, x1, hown, hraw, x2, x3, wres, acc_ref, out_v, acc2,
    mine, st_in, st_total, st_prev, mine2, st_in2, st_total2, st_prev2,
    lanes1, chans1, lanes2, chans2,
    load_sem, halo_s, halo_r, stat_s, stat_r, pair_s, pair_r,
    zs, zr, xs, xr, ps, pr,
):
    tm = lax.axis_index("tm")
    tile = lax.axis_index("tile")
    y, x = tm // NX, lax.rem(tm, NX)
    z, core = tile // 2, lax.rem(tile, 2)
    step = 1 - 2 * core
    tm_next, tm_prev = lax.rem(tm + 1, SPANS), lax.rem(tm + SPANS - 1, SPANS)
    up, down = lax.rem(tile + TILES - 1, TILES), lax.rem(tile + 1, TILES)
    partner = (tm, tile + step)

    def along_x(by):
        return (y * NX + lax.rem(x + by + 2 * NX, NX), tile)

    def along_z(by):
        return (tm, lax.rem(z + by + 2 * NZ, NZ) * 2 + core)

    def remote(src, dst, send, recv, to):
        return pltpu.make_async_remote_copy(
            src_ref=src, dst_ref=dst, send_sem=send, recv_sem=recv,
            device_id=to, device_id_type=pl.DeviceIdType.MESH,
        )

    loads = [
        pltpu.make_async_copy(lat, xraw.at[2:6, 1:5], load_sem.at[0]),
        pltpu.make_async_copy(fk, fk_in, load_sem.at[1]),
        pltpu.make_async_copy(sk, w2, load_sem.at[2]),
        pltpu.make_async_copy(skw, wskip, load_sem.at[3]),
        pltpu.make_async_copy(rk, rkv, load_sem.at[4]),
    ]
    for load in loads:
        load.start()

    barrier = pltpu.get_barrier_semaphore()
    near = [along_x(1), along_x(-1), (tm_prev, tile), (tm_prev, up), (tm_prev, down)]

    def greet(to):
        pl.semaphore_signal(barrier, inc=1, device_id=to, device_id_type=pl.DeviceIdType.MESH)

    def greet_group(i, carry):
        greet((tm, lax.rem(tile + i, TILES)))
        return carry

    lax.fori_loop(1, TILES, greet_group, 0)
    for to in near:
        greet(to)

    lanes1[...] = member(CIN // GROUPS, False)
    chans1[...] = member(CIN // GROUPS, True)
    lanes2[...] = member(CMID // GROUPS, False)
    chans2[...] = member(CMID // GROUPS, True)

    loads[0].wait()
    sums, squares = [], []
    for f in range(FR):
        v = xraw[2 + f, 1:5].astype(F32).reshape(ROWS * COLS, CIN)
        sums.append(jnp.sum(v, axis=0, keepdims=True))
        squares.append(jnp.sum(v * v, axis=0, keepdims=True))
    mine[...] = partial_stats(jnp.concatenate(sums), jnp.concatenate(squares), lanes1[...])
    loads[4].wait()
    for a in range(2):
        for tap in range(2):
            if a == 0:
                q = [rkv[0, d].astype(F32) for d in range(3)] if tap == 0 else [
                    rkv[1, d].astype(F32) + rkv[2, d].astype(F32) for d in range(3)
                ]
            else:
                q = [rkv[0, d].astype(F32) + rkv[1, d].astype(F32) for d in range(3)] if tap == 0 else [
                    rkv[2, d].astype(F32) for d in range(3)
                ]
            none = jnp.zeros_like(q[0])
            cols = [
                jnp.concatenate([q[0], none], axis=1),
                jnp.concatenate([q[1] + q[2], q[0] + q[1]], axis=1),
                jnp.concatenate([none, q[2]], axis=1),
            ]
            for d in range(3):
                wres[a, (tap * 3 + d) * CMID : (tap * 3 + d + 1) * CMID, :] = cols[d].astype(BF16)

    loads[1].wait()
    pl.semaphore_wait(barrier, TILES - 1 + len(near))

    def exchange(src, at_in, phase):
        for far in range(8, 0, -1):
            for i in (far, TILES - far)[: 2 if far < 8 else 1]:
                remote(
                    src, at_in.at[i - 1], stat_s.at[phase, 0], stat_r.at[phase, 0],
                    (tm, lax.rem(tile + i, TILES)),
                ).start()

    def exchange_copy(at_in, phase):
        return remote(at_in, at_in, stat_s.at[phase, 0], stat_r.at[phase, 0], partner)

    def relay(total, at_prev, phase):
        return remote(total, at_prev, stat_s.at[phase, 1], stat_r.at[phase, 1], (tm_next, tile))

    def halo_copies(ref, rim, phase):
        lo, hi = rim, rim + ROWS
        head, tail = (lo, lo + rim), (hi - rim, hi)
        cuts = [
            ((2, 6), head, (2, 6), (hi, hi + rim), (tm, up)),
            ((2, 6), tail, (2, 6), (0, rim), (tm, down)),
            ((4, 6), (lo, hi), (0, 2), (lo, hi), (tm_next, tile)),
            ((4, 6), head, (0, 2), (hi, hi + rim), (tm_next, up)),
            ((4, 6), tail, (0, 2), (0, rim), (tm_next, down)),
        ]
        return [
            remote(
                ref.at[a[0] : a[1], b[0] : b[1]], ref.at[c[0] : c[1], d[0] : d[1]],
                halo_s.at[phase, i], halo_r.at[phase, i], to,
            )
            for i, (a, b, c, d, to) in enumerate(cuts)
        ]

    pair = remote(fk_in, fk_pair, pair_s.at[0], pair_r.at[0], partner)
    pair.start()
    exchange(mine, st_in, 0)

    pair.wait_recv()

    def both_halves(t):
        a, b = fk_in[t].astype(F32), fk_pair[t].astype(F32)
        return jnp.concatenate([jnp.where(core == 1, b, a), jnp.where(core == 1, a, b)], axis=0)

    for p in range(14):
        even = both_halves(2 * p)
        w1[3 * p, z] = even[:, :128].astype(BF16)
        if p < 13:
            odd = both_halves(2 * p + 1)
            w1[3 * p + 1, z] = odd[:, :128].astype(BF16)
            rest = jnp.concatenate([even[:, 128:], odd[:, 128:]], axis=1)
            w1[3 * p + 2, z] = rest.astype(BF16)
        else:
            rest = jnp.concatenate([even[:, 128:], jnp.zeros_like(even[:, 128:])], axis=1)
            w1[3 * p + 1, z] = rest.astype(BF16)

    my_x = XU * x
    blocks = 4

    def chip_of(k):
        return lax.rem(z - step * (k + 1) + 2 * NZ, NZ)

    def region(unit, count, chip, half):
        first = (count + 1) // 2
        if half is not None:
            unit, count = (unit, first) if half == 0 else (unit + first, count - first)
        return w1.at[pl.ds(unit, count), chip]

    def halves(k, body):
        if k < blocks - 1:
            body(None)
        else:
            for half in (0, 1):
                pl.when(core == half)(functools.partial(body, half))

    def z_copy(k, c, half):
        if c == 0:
            source, by = (z, k + 1) if k < 2 else (chip_of(1), k - 1)
            ref = region(my_x, XU, source, half)
        else:
            ref, by = region(XT, ZT, chip_of(k - 1), half), 1
        return remote(ref, ref, zs.at[k, c], zr.at[k, c], along_z(step * by))

    def x_copy(k, hop, half):
        unit = my_x if hop != 1 else XU * lax.rem(x - step + NX, NX)
        ref = region(unit, XU, chip_of(k), half)
        return remote(ref, ref, xs.at[k, hop], xr.at[k, hop], along_x((step, step, -step)[hop]))

    def p_copy(k, i, half):
        by = (-step, -2 * step, step, 0, None)[i]
        if by is None:
            ref = region(XT, ZT, chip_of(k), half)
        else:
            ref = region(XU * lax.rem(x + by + NX, NX), XU, chip_of(k), half)
        return remote(ref, ref, ps.at[k, i], pr.at[k, i], partner)

    def z_start():
        for k in (1, 0):
            z_copy(k, 0, None).start()
        z_copy(0, 1, None).start()

    def zx_arrived(k):
        def body(half):
            z_copy(k, 0, half).wait_recv()
            x_copy(k, 0, half).start()
            x_copy(k, 2, half).start()
            p_copy(k, 3, half).start()

        if k == 1:
            z_copy(1, 0, None).wait_recv()
            halves(3, lambda half: z_copy(3, 0, half).start())
            z_copy(2, 0, None).start()
            x_copy(1, 0, None).start()
            x_copy(1, 2, None).start()
            p_copy(1, 3, None).start()
        else:
            halves(k, body)

    def zz_arrived(k):
        halves(k, lambda half: z_copy(k, 1, half).wait_recv())
        if k + 1 < blocks:
            halves(k + 1, lambda half: z_copy(k + 1, 1, half).start())
        halves(k, lambda half: p_copy(k, 4, half).start())

    def x_arrived(k, hop):
        def body(half):
            x_copy(k, hop, half).wait_recv()
            if hop == 0:
                x_copy(k, 1, half).start()
            p_copy(k, hop, half).start()

        halves(k, body)

    z_start()
    halos = halo_copies(xraw, 1, 0)
    for copy in halos:
        copy.start()

    starts_here = span_start(clips, tm)
    keep_prev = jnp.where(starts_here, 0.0, 1.0).astype(F32)
    keep_top = jnp.where(tile == 0, 0.0, 1.0).astype(F32)
    keep_bottom = jnp.where(tile == TILES - 1, 0.0, 1.0).astype(F32)

    def first_act(f, scale, shift):
        a = silu(xraw[f].astype(F32) * scale[None, None, :] + shift[None, None, :])
        if f < 2:
            a = a * keep_prev
        a = jnp.concatenate([a[0:1] * keep_top, a[1:5], a[5:6] * keep_bottom], axis=0)
        for d, part in enumerate(shifted(a)):
            x1[f, :, :, d * CIN : (d + 1) * CIN] = part.astype(BF16)

    zx_arrived(1)
    exchange_copy(st_in, 0).wait_recv()
    st_total[...] = jnp.sum(st_in[...], axis=0) + mine[...]
    relayed = relay(st_total, st_prev, 0)
    relayed.start()
    zx_arrived(0)
    zz_arrived(0)
    x_arrived(1, 0)
    x_arrived(1, 2)
    zx_arrived(3)
    zx_arrived(2)
    x_arrived(0, 0)
    x_arrived(0, 2)
    zz_arrived(1)
    for copy in halos[:2]:
        copy.wait_recv()
    gain, bias = g1[...].reshape(1, CIN), b1[...].reshape(1, CIN)
    scale, shift = affine(st_total[...], gain, bias, CIN // GROUPS, chans1[...])
    first_act(2, scale[0], shift[0])
    first_act(3, scale[1], shift[1])
    x_arrived(3, 0)
    x_arrived(3, 2)
    first_act(4, scale[2], shift[2])
    first_act(5, scale[3], shift[3])
    x_arrived(1, 1)
    x_arrived(2, 2)
    x_arrived(2, 0)
    relayed.wait_recv()
    for copy in halos[2:]:
        copy.wait_recv()
    scale, shift = affine(st_prev[...], gain, bias, CIN // GROUPS, chans1[...])
    first_act(0, scale[2], shift[2])
    first_act(1, scale[3], shift[3])
    zz_arrived(2)
    x_arrived(0, 1)
    x_arrived(3, 1)
    zz_arrived(3)
    x_arrived(2, 1)

    for k in range(blocks):
        for i in range(5):
            halves(k, lambda half: p_copy(k, i, None if half is None else 1 - half).wait_recv())

    def tap_window(t):
        s, rest = divmod(t, 9)
        dy, dx = divmod(rest, 3)
        window = x1[s : s + FR, dy : dy + ROWS, :, dx * CIN : (dx + 1) * CIN]
        return window.reshape(FR * ROWS * COLS, CIN)

    def conv1(pairs, first):
        total = [None, None] if first else [acc_ref[0], acc_ref[1]]
        for p in pairs:
            rest = w1[3 * p + (2 if p < 13 else 1)].reshape(CIN, 128)
            for odd in range(2 if p < 13 else 1):
                weights = jnp.concatenate([w1[3 * p + odd].reshape(CIN, 128), rest], axis=1)
                term = jnp.dot(tap_window(2 * p + odd), weights, preferred_element_type=F32)
                total[odd] = term if total[odd] is None else total[odd] + term
        acc_ref[0], acc_ref[1] = total

    conv1(range(14), True)

    even, odd = acc_ref[0], acc_ref[1]
    hidden = jnp.concatenate([even[:, :128] + odd[:, :128], even[:, 128:192] + odd[:, 192:]], axis=1)
    hidden = hidden.reshape(FR, ROWS * COLS, CMID)
    hown[...] = hidden.reshape(FR, ROWS, COLS, CMID)
    hraw[2:6, 2:6] = hidden.reshape(FR, ROWS, COLS, CMID).astype(BF16)
    halos2 = halo_copies(hraw, 2, 1)
    for copy in halos2:
        copy.start()
    mine2[...] = partial_stats(jnp.sum(hidden, axis=1), jnp.sum(hidden * hidden, axis=1), lanes2[...])
    exchange(mine2, st_in2, 1)

    loads[3].wait()
    loads[2].wait()
    shortcut = lax.dot_general(
        xraw[2:6].reshape(FR * 6 * COLS, CIN), wskip[...], (((1,), (1,)), ((), ())),
        preferred_element_type=F32,
    )

    exchange_copy(st_in2, 1).wait_recv()
    st_total2[...] = jnp.sum(st_in2[...], axis=0) + mine2[...]
    relayed2 = relay(st_total2, st_prev2, 1)
    relayed2.start()
    for copy in halos2[:2]:
        copy.wait_recv()

    def second_act(f, scale, shift):
        if f >= 2:
            v = jnp.concatenate(
                [hraw[f, 0:2].astype(F32), hown[f - 2], hraw[f, 6:8].astype(F32)], axis=0
            )
        else:
            v = hraw[f].astype(F32)
        a = silu(v * scale[None, None, :] + shift[None, None, :])
        if f < 2:
            a = a * keep_prev
        a = jnp.concatenate([a[0:2] * keep_top, a[2:6], a[6:8] * keep_bottom], axis=0)
        x2[f] = jnp.concatenate(shifted(a), axis=-1).astype(BF16)

    def conv2(s):
        total = None
        for dy in range(3):
            window = x2[s : s + FR, dy : dy + 6].reshape(FR * 6 * COLS, 3 * CMID)
            weights = w2[9 * s + 3 * dy : 9 * s + 3 * dy + 3].reshape(3 * CMID, CMID)
            term = jnp.dot(window, weights, preferred_element_type=F32)
            total = term if total is None else total + term
        return total

    gain, bias = g2[...].reshape(1, CMID), b2[...].reshape(1, CMID)
    scale, shift = affine(st_total2[...], gain, bias, CMID // GROUPS, chans2[...])
    for f in range(FR):
        second_act(2 + f, scale[f], shift[f])
    acc2[...] = shortcut + conv2(2)
    relayed2.wait_recv()
    for copy in halos2[2:]:
        copy.wait_recv()
    scale, shift = affine(st_prev2[...], gain, bias, CMID // GROUPS, chans2[...])
    second_act(0, scale[2], shift[2])
    second_act(1, scale[3], shift[3])

    total = acc2[...] + conv2(1) + conv2(0)
    block = total.astype(BF16).astype(F32).reshape(FR, 6, COLS, CMID)
    for f in range(FR):
        a = jnp.concatenate(
            [block[f, 0:1] * keep_top, block[f, 1:5], block[f, 5:6] * keep_bottom], axis=0
        )
        x3[f] = jnp.concatenate(shifted(a), axis=-1).astype(BF16)

    for a in range(2):
        window = jnp.concatenate(
            [x3[:, a : a + ROWS], x3[:, a + 1 : a + 1 + ROWS]], axis=-1
        ).reshape(FR * ROWS * COLS, 6 * CMID)
        res = jnp.dot(window, wres[a], preferred_element_type=F32)
        res = res.astype(BF16).reshape(FR, ROWS, COLS, 2 * COUT)
        out_v[:, :, a] = res
    store = pltpu.make_async_copy(out_v, out, load_sem.at[5])
    store.start()

    pair.wait_send()
    for copy in halos + halos2:
        copy.wait_send()
    for copy in (exchange_copy(st_in, 0), exchange_copy(st_in2, 1), relayed, relayed2):
        copy.wait_send()

    def drain(k, half):
        for c in range(2):
            z_copy(k, c, half).wait_send()
        for hop in range(3):
            x_copy(k, hop, half).wait_send()
        for i in range(5):
            p_copy(k, i, half).wait_send()

    for k in range(blocks):
        halves(k, functools.partial(drain, k))
    store.wait()


def span_start(clips, tm):
    start, hit = jnp.int32(0), tm == 0
    for j in range(3):
        start = start + clips[j]
        hit = hit | (start == tm)
    return hit


def shards(
    latents, first_gain, first_bias, first_kernel, second_gain, second_bias,
    second_kernel, skip_weight, resample_kernel, clip_spans,
):
    fk = jnp.transpose(first_kernel, (1, 2, 3, 0, 4)).reshape(27, SHARD, CMID)
    sk = jnp.transpose(second_kernel, (1, 2, 3, 0, 4)).reshape(27, CMID, CMID)
    anywhere = pl.BlockSpec(memory_space=pl.ANY)
    vmem = pl.BlockSpec(memory_space=pltpu.VMEM)
    smem = pl.BlockSpec(memory_space=pltpu.SMEM)
    dma = pltpu.SemaphoreType.DMA
    out = pl.pallas_call(
        kernel,
        out_shape=jax.ShapeDtypeStruct((FR, ROWS, 2, COLS, 2 * COUT), BF16),
        in_specs=[anywhere, vmem, vmem, anywhere, vmem, vmem, anywhere, anywhere, anywhere, smem],
        out_specs=anywhere,
        scratch_shapes=[
            pltpu.VMEM((6, 6, COLS, CIN), BF16),
            pltpu.VMEM((27, SHARD, CMID), BF16),
            pltpu.VMEM((27, SHARD, CMID), BF16),
            pltpu.VMEM((UNITS, NZ, UNIT, 128), BF16),
            pltpu.VMEM((27, CMID, CMID), BF16),
            pltpu.VMEM((CMID, CIN), BF16),
            pltpu.VMEM((3, 3, CMID, COUT), BF16),
            pltpu.VMEM((6, 6, COLS, 3 * CIN), BF16),
            pltpu.VMEM((FR, ROWS, COLS, CMID), F32),
            pltpu.VMEM((6, 8, COLS, CMID), BF16),
            pltpu.VMEM((6, 8, COLS, 3 * CMID), BF16),
            pltpu.VMEM((FR, 6, COLS, 3 * CMID), BF16),
            pltpu.VMEM((2, 6 * CMID, 2 * COUT), BF16),
            pltpu.VMEM((2, FR * ROWS * COLS, 256), F32),
            pltpu.VMEM((FR, ROWS, 2, COLS, 2 * COUT), BF16),
            pltpu.VMEM((FR * 6 * COLS, CMID), F32),
            pltpu.VMEM((2, 128), F32),
            pltpu.VMEM((TILES - 1, 2, 128), F32),
            pltpu.VMEM((2, 128), F32),
            pltpu.VMEM((2, 128), F32),
            pltpu.VMEM((2, 128), F32),
            pltpu.VMEM((TILES - 1, 2, 128), F32),
            pltpu.VMEM((2, 128), F32),
            pltpu.VMEM((2, 128), F32),
            pltpu.VMEM((CIN, 128), BF16),
            pltpu.VMEM((128, CIN), BF16),
            pltpu.VMEM((CMID, 128), BF16),
            pltpu.VMEM((128, CMID), BF16),
            dma((6,)),
            dma((2, 5)), dma((2, 5)),
            dma((2, 2)), dma((2, 2)),
            dma((1,)), dma((1,)),
            dma((4, 2)), dma((4, 2)),
            dma((4, 3)), dma((4, 3)),
            dma((4, 5)), dma((4, 5)),
        ],
        compiler_params=pltpu.CompilerParams(
            collective_id=0, has_side_effects=True, vmem_limit_bytes=56 * 2**20
        ),
    )(
        latents, first_gain, first_bias, fk,
        second_gain, second_bias, sk, skip_weight.T,
        resample_kernel, clip_spans,
    )
    return out.reshape(FR, 2 * ROWS, COLS, 2 * COUT)


def solution(mesh):
    in_specs = (
        P("tm", "tile", None, None), P(), P(), P("tile", None, None, None, None),
        P(), P(), P(), P(), P(), P(),
    )
    return jax.shard_map(
        shards, mesh=mesh, in_specs=in_specs, out_specs=P("tm", "tile", None, None), check_vma=False
    )
```

```python
import functools

import jax
import jax.numpy as jnp
from jax import lax
from jax.experimental import pallas as pl
from jax.experimental.pallas import tpu as pltpu
from jax.sharding import PartitionSpec as P

GROUPS = 32
EPS = 1e-6
F32 = jnp.float32
BF16 = jnp.bfloat16

FR, ROWS, COLS = 4, 4, 16
CIN, CMID, COUT = 384, 192, 96
SPANS, TILES = 32, 16
NX, NY, NZ = 4, 8, 8
SHARD = CIN // TILES
UNIT = 2 * SHARD
UNITS = 41
XU, YU = 4, 2
XT, YT = XU * NX, YU * NY
ZT = UNITS - XT - YT
PAD = 256
HEIGHT = ROWS * TILES


def member(per, transposed):
    channels = per * GROUPS
    shape = (128, channels) if transposed else (channels, 128)
    lane = lax.broadcasted_iota(jnp.int32, shape, 0 if transposed else 1)
    chan = lax.broadcasted_iota(jnp.int32, shape, 1 if transposed else 0)
    first = jnp.bitwise_and(lane, GROUPS - 1) * per
    return jnp.where((chan >= first) & (chan < first + per), 1.0, 0.0).astype(BF16)


def frame_lanes(rows):
    lane = lax.broadcasted_iota(jnp.int32, (rows, 128), 1)
    row = lax.broadcasted_iota(jnp.int32, (rows, 128), 0)
    low = jnp.bitwise_and(row, FR - 1) * GROUPS
    return (lane >= low) & (lane < low + GROUPS)


def exact_dot(values, zero_one):
    rows = values.shape[0]
    high = values.astype(BF16).astype(F32)
    left = values - high
    middle = left.astype(BF16).astype(F32)
    terms = jnp.concatenate([high, middle, left - middle], axis=0).astype(BF16)
    wide = jnp.dot(terms, zero_one, preferred_element_type=F32)
    return wide[:rows] + wide[rows : 2 * rows] + wide[2 * rows :]


def partial_stats(sums, squares, to_lanes):
    wide = exact_dot(jnp.concatenate([sums, squares], axis=0), to_lanes)
    wide = jnp.where(frame_lanes(2 * FR), wide, 0.0)
    return jnp.concatenate(
        [jnp.sum(wide[:FR], axis=0, keepdims=True), jnp.sum(wide[FR:], axis=0, keepdims=True)], axis=0
    )


def affine(message, gain, bias, per, to_channels):
    entries = float(HEIGHT * COLS * per)
    mean = message[0:1] / entries
    inv = lax.rsqrt(message[1:2] / entries - mean * mean + EPS)
    stacked = jnp.concatenate([jnp.broadcast_to(mean, (FR, 128)), jnp.broadcast_to(inv, (FR, 128))], axis=0)
    wide = exact_dot(jnp.where(frame_lanes(2 * FR), stacked, 0.0), to_channels)
    scale = wide[FR:] * gain
    return scale, bias - wide[:FR] * scale


def silu(v):
    half = 0.5 * v
    return half + half * jnp.tanh(half)


def shifted(a):
    zero = jnp.zeros(a.shape[:1] + (1,) + a.shape[2:], a.dtype)
    left = jnp.concatenate([zero, a[:, : COLS - 1]], axis=1)
    right = jnp.concatenate([a[:, 1:], zero], axis=1)
    return left, a, right


def kernel(
    lat, g1, b1, fk, g2, b2, sk, skw, rk, clips, out,
    xraw, fk_in, fk_pair, w1, wy, w2, wskip, rkv, x1, hown, hraw, x2, x3, wres, acc_ref, out_v, acc2,
    mine, st_in, st_total, st_prev, mine2, st_in2, st_total2, st_prev2,
    lanes1, chans1, lanes2, chans2,
    load_sem, halo_s, halo_r, stat_s, stat_r, pair_s, pair_r,
    zs, zr, xs, xr, ys, yr, ps, pr,
):
    tm = lax.axis_index("tm")
    tile = lax.axis_index("tile")
    y, x = tm // NX, lax.rem(tm, NX)
    z, core = tile // 2, lax.rem(tile, 2)
    step = 1 - 2 * core
    tm_next, tm_prev = lax.rem(tm + 1, SPANS), lax.rem(tm + SPANS - 1, SPANS)
    up, down = lax.rem(tile + TILES - 1, TILES), lax.rem(tile + 1, TILES)
    partner = (tm, tile + step)

    def along_x(by):
        return (y * NX + lax.rem(x + by + 2 * NX, NX), tile)

    def along_y(by):
        return (lax.rem(y + by + 2 * NY, NY) * NX + x, tile)

    def along_z(by):
        return (tm, lax.rem(z + by + 2 * NZ, NZ) * 2 + core)

    def remote(src, dst, send, recv, to):
        return pltpu.make_async_remote_copy(
            src_ref=src, dst_ref=dst, send_sem=send, recv_sem=recv,
            device_id=to, device_id_type=pl.DeviceIdType.MESH,
        )

    loads = [
        pltpu.make_async_copy(lat, xraw.at[2:6, 1:5], load_sem.at[0]),
        pltpu.make_async_copy(fk, fk_in, load_sem.at[1]),
        pltpu.make_async_copy(sk, w2, load_sem.at[2]),
        pltpu.make_async_copy(skw, wskip, load_sem.at[3]),
        pltpu.make_async_copy(rk, rkv, load_sem.at[4]),
    ]
    for load in loads:
        load.start()

    barrier = pltpu.get_barrier_semaphore()
    near = [along_x(1), along_x(-1), along_y(1), along_y(-1), along_y(2), along_y(-2)]
    near += [(tm_prev, tile), (tm_prev, up), (tm_prev, down)]

    def greet(to):
        pl.semaphore_signal(barrier, inc=1, device_id=to, device_id_type=pl.DeviceIdType.MESH)

    def greet_group(i, carry):
        greet((tm, lax.rem(tile + i, TILES)))
        return carry

    lax.fori_loop(1, TILES, greet_group, 0)
    for to in near:
        greet(to)

    lanes1[...] = member(CIN // GROUPS, False)
    chans1[...] = member(CIN // GROUPS, True)
    lanes2[...] = member(CMID // GROUPS, False)
    chans2[...] = member(CMID // GROUPS, True)

    loads[0].wait()
    sums, squares = [], []
    for f in range(FR):
        v = xraw[2 + f, 1:5].astype(F32).reshape(ROWS * COLS, CIN)
        sums.append(jnp.sum(v, axis=0, keepdims=True))
        squares.append(jnp.sum(v * v, axis=0, keepdims=True))
    mine[...] = partial_stats(jnp.concatenate(sums), jnp.concatenate(squares), lanes1[...])
    loads[4].wait()
    for a in range(2):
        for tap in range(2):
            if a == 0:
                q = [rkv[0, d].astype(F32) for d in range(3)] if tap == 0 else [
                    rkv[1, d].astype(F32) + rkv[2, d].astype(F32) for d in range(3)
                ]
            else:
                q = [rkv[0, d].astype(F32) + rkv[1, d].astype(F32) for d in range(3)] if tap == 0 else [
                    rkv[2, d].astype(F32) for d in range(3)
                ]
            none = jnp.zeros_like(q[0])
            cols = [
                jnp.concatenate([q[0], none], axis=1),
                jnp.concatenate([q[1] + q[2], q[0] + q[1]], axis=1),
                jnp.concatenate([none, q[2]], axis=1),
            ]
            for d in range(3):
                wres[a, (tap * 3 + d) * CMID : (tap * 3 + d + 1) * CMID, :] = cols[d].astype(BF16)

    loads[1].wait()
    pl.semaphore_wait(barrier, TILES - 1 + len(near))

    def exchange(src, at_in, phase):
        for far in range(8, 0, -1):
            for i in (far, TILES - far)[: 2 if far < 8 else 1]:
                remote(
                    src, at_in.at[i - 1], stat_s.at[phase, 0], stat_r.at[phase, 0],
                    (tm, lax.rem(tile + i, TILES)),
                ).start()

    def exchange_copy(at_in, phase):
        return remote(at_in, at_in, stat_s.at[phase, 0], stat_r.at[phase, 0], partner)

    def relay(total, at_prev, phase):
        return remote(total, at_prev, stat_s.at[phase, 1], stat_r.at[phase, 1], (tm_next, tile))

    def halo_copies(ref, rim, phase):
        lo, hi = rim, rim + ROWS
        head, tail = (lo, lo + rim), (hi - rim, hi)
        cuts = [
            ((2, 6), head, (2, 6), (hi, hi + rim), (tm, up)),
            ((2, 6), tail, (2, 6), (0, rim), (tm, down)),
            ((4, 6), (lo, hi), (0, 2), (lo, hi), (tm_next, tile)),
            ((4, 6), head, (0, 2), (hi, hi + rim), (tm_next, up)),
            ((4, 6), tail, (0, 2), (0, rim), (tm_next, down)),
        ]
        return [
            remote(
                ref.at[a[0] : a[1], b[0] : b[1]], ref.at[c[0] : c[1], d[0] : d[1]],
                halo_s.at[phase, i], halo_r.at[phase, i], to,
            )
            for i, (a, b, c, d, to) in enumerate(cuts)
        ]

    pair = remote(fk_in, fk_pair, pair_s.at[0], pair_r.at[0], partner)
    pair.start()
    exchange(mine, st_in, 0)

    pair.wait_recv()

    def unit_ref(u):
        if XT <= u < XT + YT:
            return wy.at[(u - XT) // YU, (u - XT) % YU]
        return w1.at[u]

    def both_halves(t):
        a, b = fk_in[t].astype(F32), fk_pair[t].astype(F32)
        return jnp.concatenate([jnp.where(core == 1, b, a), jnp.where(core == 1, a, b)], axis=0)

    for p in range(14):
        even = both_halves(2 * p)
        unit_ref(3 * p)[z] = even[:, :128].astype(BF16)
        if p < 13:
            odd = both_halves(2 * p + 1)
            unit_ref(3 * p + 1)[z] = odd[:, :128].astype(BF16)
            rest = jnp.concatenate([even[:, 128:], odd[:, 128:]], axis=1)
            unit_ref(3 * p + 2)[z] = rest.astype(BF16)
        else:
            rest = jnp.concatenate([even[:, 128:], jnp.zeros_like(even[:, 128:])], axis=1)
            unit_ref(3 * p + 1)[z] = rest.astype(BF16)

    my_x = XU * x
    blocks = 4

    def chip_of(k):
        return lax.rem(z - step * (k + 1) + 2 * NZ, NZ)

    def region(unit, count, chip, half):
        first = (count + 1) // 2
        if half is not None:
            unit, count = (unit, first) if half == 0 else (unit + first, count - first)
        return w1.at[pl.ds(unit, count), chip]

    def y_region(at, chip, half):
        return wy.at[at, :, chip] if half is None else wy.at[at, half, chip]

    def halves(k, body):
        if k < blocks - 1:
            body(None)
        else:
            for half in (0, 1):
                pl.when(core == half)(functools.partial(body, half))

    def z_copy(k, c, half):
        if c < 2:
            ref = region(my_x, XU, z, half) if c == 0 else y_region(y, z, half)
            by = k + 1
        else:
            ref = region(XT + YT, ZT, z if k < 2 else chip_of(1), half)
            by = k + 1 if k < 2 else k - 1
        return remote(ref, ref, zs.at[k, c], zr.at[k, c], along_z(step * by))

    def x_copy(k, hop, half):
        unit = my_x if hop != 1 else XU * lax.rem(x - step + NX, NX)
        ref = region(unit, XU, chip_of(k), half)
        return remote(ref, ref, xs.at[k, hop], xr.at[k, hop], along_x((step, step, -step)[hop]))

    def y_copy(k, hop, half):
        origin = {2: -2 * step, 3: -2 * step, 6: 2 * step}.get(hop, 0)
        by = (step, 2 * step, step, 2 * step, -step, -2 * step, -step)[hop]
        ref = y_region(lax.rem(y + origin + NY, NY), chip_of(k), half)
        return remote(ref, ref, ys.at[k, hop], yr.at[k, hop], along_y(by))

    def p_copy(k, i, half):
        if i < 4:
            by = (-step, -2 * step, step, 0)[i]
            ref = region(XU * lax.rem(x + by + NX, NX), XU, chip_of(k), half)
        elif i == 5:
            ref = region(XT + YT, ZT, chip_of(k), half)
        else:
            ref = y_region(slice(None), chip_of(k), half)
        return remote(ref, ref, ps.at[k, i], pr.at[k, i], partner)

    def z_start():
        for c in (1, 0):
            for k in range(blocks):
                halves(k, lambda half: z_copy(k, c, half).start())
        for k in (1, 0):
            z_copy(k, 2, None).start()

    def zy_arrived(k):
        def body(half):
            z_copy(k, 1, half).wait_recv()
            for hop in (1, 5, 0, 4):
                y_copy(k, hop, half).start()

        halves(k, body)

    def zx_arrived(k):
        def body(half):
            z_copy(k, 0, half).wait_recv()
            x_copy(k, 0, half).start()
            x_copy(k, 2, half).start()
            p_copy(k, 3, half).start()

        halves(k, body)

    def zz_arrived(k):
        halves(k, lambda half: z_copy(k, 2, half).wait_recv())
        if k == 1:
            halves(3, lambda half: z_copy(3, 2, half).start())
            z_copy(2, 2, None).start()
        halves(k, lambda half: p_copy(k, 5, half).start())

    def y_arrived(k):
        def body(half):
            for hop in (0, 4):
                y_copy(k, hop, half).wait_recv()
            y_copy(k, 1, half).wait_recv()
            y_copy(k, 3, half).start()
            y_copy(k, 2, half).start()
            y_copy(k, 5, half).wait_recv()
            y_copy(k, 6, half).start()

        halves(k, body)

    def y_last(k):
        def body(half):
            for hop in (6, 2, 3):
                y_copy(k, hop, half).wait_recv()
            p_copy(k, 4, half).start()

        halves(k, body)

    def x_arrived(k, hop):
        def body(half):
            x_copy(k, hop, half).wait_recv()
            if hop == 0:
                x_copy(k, 1, half).start()
            p_copy(k, hop, half).start()

        halves(k, body)

    z_start()
    halos = halo_copies(xraw, 1, 0)
    for copy in halos:
        copy.start()

    starts_here = span_start(clips, tm)
    keep_prev = jnp.where(starts_here, 0.0, 1.0).astype(F32)
    keep_top = jnp.where(tile == 0, 0.0, 1.0).astype(F32)
    keep_bottom = jnp.where(tile == TILES - 1, 0.0, 1.0).astype(F32)

    def first_act(f, scale, shift):
        a = silu(xraw[f].astype(F32) * scale[None, None, :] + shift[None, None, :])
        if f < 2:
            a = a * keep_prev
        a = jnp.concatenate([a[0:1] * keep_top, a[1:5], a[5:6] * keep_bottom], axis=0)
        for d, part in enumerate(shifted(a)):
            x1[f, :, :, d * CIN : (d + 1) * CIN] = part.astype(BF16)

    zy_arrived(0)
    zy_arrived(1)
    zy_arrived(2)
    exchange_copy(st_in, 0).wait_recv()
    st_total[...] = jnp.sum(st_in[...], axis=0) + mine[...]
    relayed = relay(st_total, st_prev, 0)
    relayed.start()
    zx_arrived(0)
    zy_arrived(3)
    zx_arrived(1)
    y_arrived(0)
    zx_arrived(2)
    y_arrived(1)
    x_arrived(0, 0)
    x_arrived(0, 2)
    y_arrived(2)
    zx_arrived(3)
    x_arrived(1, 0)
    x_arrived(1, 2)
    zz_arrived(1)
    y_arrived(3)
    for copy in halos[:2]:
        copy.wait_recv()
    gain, bias = g1[...].reshape(1, CIN), b1[...].reshape(1, CIN)
    scale, shift = affine(st_total[...], gain, bias, CIN // GROUPS, chans1[...])
    first_act(2, scale[0], shift[0])
    first_act(3, scale[1], shift[1])
    x_arrived(2, 0)
    x_arrived(2, 2)
    y_last(0)
    zz_arrived(0)
    first_act(4, scale[2], shift[2])
    first_act(5, scale[3], shift[3])
    x_arrived(0, 1)
    y_last(1)
    x_arrived(3, 0)
    x_arrived(3, 2)
    relayed.wait_recv()
    for copy in halos[2:]:
        copy.wait_recv()
    scale, shift = affine(st_prev[...], gain, bias, CIN // GROUPS, chans1[...])
    first_act(0, scale[2], shift[2])
    y_last(2)
    x_arrived(1, 1)
    first_act(1, scale[3], shift[3])
    y_last(3)
    zz_arrived(3)
    x_arrived(2, 1)
    zz_arrived(2)
    x_arrived(3, 1)

    def partner_wait(parts):
        for k in range(blocks):
            for i in parts:
                halves(k, lambda half: p_copy(k, i, None if half is None else 1 - half).wait_recv())

    def tap_window(t):
        s, rest = divmod(t, 9)
        dy, dx = divmod(rest, 3)
        window = x1[s : s + FR, dy : dy + ROWS, :, dx * CIN : (dx + 1) * CIN]
        return window.reshape(FR * ROWS * COLS, CIN)

    def conv1(pairs, first):
        total = [None, None] if first else [acc_ref[0], acc_ref[1]]
        for p in pairs:
            rest = unit_ref(3 * p + (2 if p < 13 else 1))[...].reshape(CIN, 128)
            for odd in range(2 if p < 13 else 1):
                weights = jnp.concatenate([unit_ref(3 * p + odd)[...].reshape(CIN, 128), rest], axis=1)
                term = jnp.dot(tap_window(2 * p + odd), weights, preferred_element_type=F32)
                total[odd] = term if total[odd] is None else total[odd] + term
        acc_ref[0], acc_ref[1] = total

    partner_wait((4, 5))
    conv1(range(6, 14), True)
    partner_wait((0, 1, 2, 3))
    conv1(range(0, 6), False)

    even, odd = acc_ref[0], acc_ref[1]
    hidden = jnp.concatenate([even[:, :128] + odd[:, :128], even[:, 128:192] + odd[:, 192:]], axis=1)
    hidden = hidden.reshape(FR, ROWS * COLS, CMID)
    hown[...] = hidden.reshape(FR, ROWS, COLS, CMID)
    hraw[2:6, 2:6] = hidden.reshape(FR, ROWS, COLS, CMID).astype(BF16)
    halos2 = halo_copies(hraw, 2, 1)
    for copy in halos2:
        copy.start()
    mine2[...] = partial_stats(jnp.sum(hidden, axis=1), jnp.sum(hidden * hidden, axis=1), lanes2[...])
    exchange(mine2, st_in2, 1)

    loads[3].wait()
    loads[2].wait()
    shortcut = lax.dot_general(
        xraw[2:6].reshape(FR * 6 * COLS, CIN), wskip[...], (((1,), (1,)), ((), ())),
        preferred_element_type=F32,
    )

    exchange_copy(st_in2, 1).wait_recv()
    st_total2[...] = jnp.sum(st_in2[...], axis=0) + mine2[...]
    relayed2 = relay(st_total2, st_prev2, 1)
    relayed2.start()
    for copy in halos2[:2]:
        copy.wait_recv()

    def second_act(f, scale, shift):
        if f >= 2:
            v = jnp.concatenate(
                [hraw[f, 0:2].astype(F32), hown[f - 2], hraw[f, 6:8].astype(F32)], axis=0
            )
        else:
            v = hraw[f].astype(F32)
        a = silu(v * scale[None, None, :] + shift[None, None, :])
        if f < 2:
            a = a * keep_prev
        a = jnp.concatenate([a[0:2] * keep_top, a[2:6], a[6:8] * keep_bottom], axis=0)
        x2[f] = jnp.concatenate(shifted(a), axis=-1).astype(BF16)

    def conv2(s):
        total = None
        for dy in range(3):
            window = x2[s : s + FR, dy : dy + 6].reshape(FR * 6 * COLS, 3 * CMID)
            weights = w2[9 * s + 3 * dy : 9 * s + 3 * dy + 3].reshape(3 * CMID, CMID)
            term = jnp.dot(window, weights, preferred_element_type=F32)
            total = term if total is None else total + term
        return total

    gain, bias = g2[...].reshape(1, CMID), b2[...].reshape(1, CMID)
    scale, shift = affine(st_total2[...], gain, bias, CMID // GROUPS, chans2[...])
    for f in range(FR):
        second_act(2 + f, scale[f], shift[f])
    acc2[...] = shortcut + conv2(2)
    relayed2.wait_recv()
    for copy in halos2[2:]:
        copy.wait_recv()
    scale, shift = affine(st_prev2[...], gain, bias, CMID // GROUPS, chans2[...])
    second_act(0, scale[2], shift[2])
    second_act(1, scale[3], shift[3])

    total = acc2[...] + conv2(1) + conv2(0)
    block = total.astype(BF16).astype(F32).reshape(FR, 6, COLS, CMID)
    for f in range(FR):
        a = jnp.concatenate(
            [block[f, 0:1] * keep_top, block[f, 1:5], block[f, 5:6] * keep_bottom], axis=0
        )
        x3[f] = jnp.concatenate(shifted(a), axis=-1).astype(BF16)

    for a in range(2):
        window = jnp.concatenate(
            [x3[:, a : a + ROWS], x3[:, a + 1 : a + 1 + ROWS]], axis=-1
        ).reshape(FR * ROWS * COLS, 6 * CMID)
        res = jnp.dot(window, wres[a], preferred_element_type=F32)
        res = res.astype(BF16).reshape(FR, ROWS, COLS, 2 * COUT)
        out_v[:, :, a] = res
    store = pltpu.make_async_copy(out_v, out, load_sem.at[5])
    store.start()

    pair.wait_send()
    for copy in halos + halos2:
        copy.wait_send()
    for copy in (exchange_copy(st_in, 0), exchange_copy(st_in2, 1), relayed, relayed2):
        copy.wait_send()

    def drain(k, half):
        for c in range(3):
            z_copy(k, c, half).wait_send()
        for hop in range(3):
            x_copy(k, hop, half).wait_send()
        for hop in range(7):
            y_copy(k, hop, half).wait_send()
        for i in range(6):
            p_copy(k, i, half).wait_send()

    for k in range(blocks):
        halves(k, functools.partial(drain, k))
    store.wait()


def span_start(clips, tm):
    start, hit = jnp.int32(0), tm == 0
    for j in range(3):
        start = start + clips[j]
        hit = hit | (start == tm)
    return hit


def shards(
    latents, first_gain, first_bias, first_kernel, second_gain, second_bias,
    second_kernel, skip_weight, resample_kernel, clip_spans,
):
    fk = jnp.transpose(first_kernel, (1, 2, 3, 0, 4)).reshape(27, SHARD, CMID)
    sk = jnp.transpose(second_kernel, (1, 2, 3, 0, 4)).reshape(27, CMID, CMID)
    anywhere = pl.BlockSpec(memory_space=pl.ANY)
    vmem = pl.BlockSpec(memory_space=pltpu.VMEM)
    smem = pl.BlockSpec(memory_space=pltpu.SMEM)
    dma = pltpu.SemaphoreType.DMA
    out = pl.pallas_call(
        kernel,
        out_shape=jax.ShapeDtypeStruct((FR, ROWS, 2, COLS, 2 * COUT), BF16),
        in_specs=[anywhere, vmem, vmem, anywhere, vmem, vmem, anywhere, anywhere, anywhere, smem],
        out_specs=anywhere,
        scratch_shapes=[
            pltpu.VMEM((6, 6, COLS, CIN), BF16),
            pltpu.VMEM((27, SHARD, CMID), BF16),
            pltpu.VMEM((27, SHARD, CMID), BF16),
            pltpu.VMEM((UNITS, NZ, UNIT, 128), BF16),
            pltpu.VMEM((NY, YU, NZ, UNIT, 128), BF16),
            pltpu.VMEM((27, CMID, CMID), BF16),
            pltpu.VMEM((CMID, CIN), BF16),
            pltpu.VMEM((3, 3, CMID, COUT), BF16),
            pltpu.VMEM((6, 6, COLS, 3 * CIN), BF16),
            pltpu.VMEM((FR, ROWS, COLS, CMID), F32),
            pltpu.VMEM((6, 8, COLS, CMID), BF16),
            pltpu.VMEM((6, 8, COLS, 3 * CMID), BF16),
            pltpu.VMEM((FR, 6, COLS, 3 * CMID), BF16),
            pltpu.VMEM((2, 6 * CMID, 2 * COUT), BF16),
            pltpu.VMEM((2, FR * ROWS * COLS, 256), F32),
            pltpu.VMEM((FR, ROWS, 2, COLS, 2 * COUT), BF16),
            pltpu.VMEM((FR * 6 * COLS, CMID), F32),
            pltpu.VMEM((2, 128), F32),
            pltpu.VMEM((TILES - 1, 2, 128), F32),
            pltpu.VMEM((2, 128), F32),
            pltpu.VMEM((2, 128), F32),
            pltpu.VMEM((2, 128), F32),
            pltpu.VMEM((TILES - 1, 2, 128), F32),
            pltpu.VMEM((2, 128), F32),
            pltpu.VMEM((2, 128), F32),
            pltpu.VMEM((CIN, 128), BF16),
            pltpu.VMEM((128, CIN), BF16),
            pltpu.VMEM((CMID, 128), BF16),
            pltpu.VMEM((128, CMID), BF16),
            dma((6,)),
            dma((2, 5)), dma((2, 5)),
            dma((2, 2)), dma((2, 2)),
            dma((1,)), dma((1,)),
            dma((4, 3)), dma((4, 3)),
            dma((4, 3)), dma((4, 3)),
            dma((4, 7)), dma((4, 7)),
            dma((4, 6)), dma((4, 6)),
        ],
        compiler_params=pltpu.CompilerParams(
            collective_id=0, has_side_effects=True, vmem_limit_bytes=56 * 2**20
        ),
    )(
        latents, first_gain, first_bias, fk,
        second_gain, second_bias, sk, skip_weight.T,
        resample_kernel, clip_spans,
    )
    return out.reshape(FR, 2 * ROWS, COLS, 2 * COUT)


def solution(mesh):
    in_specs = (
        P("tm", "tile", None, None), P(), P(), P("tile", None, None, None, None),
        P(), P(), P(), P(), P(), P(),
    )
    return jax.shard_map(
        shards, mesh=mesh, in_specs=in_specs, out_specs=P("tm", "tile", None, None), check_vma=False
    )
```

```python
import functools

import jax
import jax.numpy as jnp
from jax import lax
from jax.experimental import pallas as pl
from jax.experimental.pallas import tpu as pltpu
from jax.sharding import PartitionSpec as P

GROUPS = 32
EPS = 1e-6
F32 = jnp.float32
BF16 = jnp.bfloat16

FR, ROWS, COLS = 4, 4, 16
CIN, CMID, COUT = 384, 192, 96
SPANS, TILES = 32, 16
NX, NY, NZ = 4, 8, 8
SHARD = CIN // TILES
UNIT = 2 * SHARD
UNITS = 41
XU, YU = 4, 2
XT, YT = XU * NX, YU * NY
ZT = UNITS - XT - YT
PAD = 256
HEIGHT = ROWS * TILES


def member(per, transposed):
    channels = per * GROUPS
    shape = (128, channels) if transposed else (channels, 128)
    lane = lax.broadcasted_iota(jnp.int32, shape, 0 if transposed else 1)
    chan = lax.broadcasted_iota(jnp.int32, shape, 1 if transposed else 0)
    first = jnp.bitwise_and(lane, GROUPS - 1) * per
    return jnp.where((chan >= first) & (chan < first + per), 1.0, 0.0).astype(BF16)


def frame_lanes(rows):
    lane = lax.broadcasted_iota(jnp.int32, (rows, 128), 1)
    row = lax.broadcasted_iota(jnp.int32, (rows, 128), 0)
    low = jnp.bitwise_and(row, FR - 1) * GROUPS
    return (lane >= low) & (lane < low + GROUPS)


def exact_dot(values, zero_one):
    rows = values.shape[0]
    high = values.astype(BF16).astype(F32)
    left = values - high
    middle = left.astype(BF16).astype(F32)
    terms = jnp.concatenate([high, middle, left - middle], axis=0).astype(BF16)
    wide = jnp.dot(terms, zero_one, preferred_element_type=F32)
    return wide[:rows] + wide[rows : 2 * rows] + wide[2 * rows :]


def partial_stats(sums, squares, to_lanes):
    wide = exact_dot(jnp.concatenate([sums, squares], axis=0), to_lanes)
    wide = jnp.where(frame_lanes(2 * FR), wide, 0.0)
    return jnp.concatenate(
        [jnp.sum(wide[:FR], axis=0, keepdims=True), jnp.sum(wide[FR:], axis=0, keepdims=True)], axis=0
    )


def affine(message, gain, bias, per, to_channels):
    entries = float(HEIGHT * COLS * per)
    mean = message[0:1] / entries
    inv = lax.rsqrt(message[1:2] / entries - mean * mean + EPS)
    stacked = jnp.concatenate([jnp.broadcast_to(mean, (FR, 128)), jnp.broadcast_to(inv, (FR, 128))], axis=0)
    wide = exact_dot(jnp.where(frame_lanes(2 * FR), stacked, 0.0), to_channels)
    scale = wide[FR:] * gain
    return scale, bias - wide[:FR] * scale


def silu(v):
    half = 0.5 * v
    return half + half * jnp.tanh(half)


def shifted(a):
    zero = jnp.zeros(a.shape[:1] + (1,) + a.shape[2:], a.dtype)
    left = jnp.concatenate([zero, a[:, : COLS - 1]], axis=1)
    right = jnp.concatenate([a[:, 1:], zero], axis=1)
    return left, a, right


def kernel(
    lat, g1, b1, fk, g2, b2, sk, skw, rk, clips, out,
    xraw, fk_in, fk_pair, w1, wy, w2, wskip, rkv, x1, hown, hraw, x2, x3, wres, acc_ref, out_v, acc2,
    mine, st_in, st_total, st_prev, mine2, st_in2, st_total2, st_prev2,
    lanes1, chans1, lanes2, chans2,
    load_sem, halo_s, halo_r, stat_s, stat_r, pair_s, pair_r,
    zs, zr, xs, xr, ys, yr, ps, pr,
):
    tm = lax.axis_index("tm")
    tile = lax.axis_index("tile")
    y, x = tm // NX, lax.rem(tm, NX)
    z, core = tile // 2, lax.rem(tile, 2)
    step = 1 - 2 * core
    tm_next, tm_prev = lax.rem(tm + 1, SPANS), lax.rem(tm + SPANS - 1, SPANS)
    up, down = lax.rem(tile + TILES - 1, TILES), lax.rem(tile + 1, TILES)
    partner = (tm, tile + step)

    def along_x(by):
        return (y * NX + lax.rem(x + by + 2 * NX, NX), tile)

    def along_y(by):
        return (lax.rem(y + by + 2 * NY, NY) * NX + x, tile)

    def along_z(by):
        return (tm, lax.rem(z + by + 2 * NZ, NZ) * 2 + core)

    def remote(src, dst, send, recv, to):
        return pltpu.make_async_remote_copy(
            src_ref=src, dst_ref=dst, send_sem=send, recv_sem=recv,
            device_id=to, device_id_type=pl.DeviceIdType.MESH,
        )

    loads = [
        pltpu.make_async_copy(lat, xraw.at[2:6, 1:5], load_sem.at[0]),
        pltpu.make_async_copy(fk, fk_in, load_sem.at[1]),
        pltpu.make_async_copy(sk, w2.at[:, :CMID], load_sem.at[2]),
        pltpu.make_async_copy(skw, wskip, load_sem.at[3]),
        pltpu.make_async_copy(rk, rkv, load_sem.at[4]),
    ]
    for load in loads:
        load.start()

    barrier = pltpu.get_barrier_semaphore()
    near = [along_x(1), along_x(-1), along_y(1), along_y(-1), along_y(2), along_y(-2)]
    near += [(tm_prev, tile), (tm_prev, up), (tm_prev, down)]

    def greet(to):
        pl.semaphore_signal(barrier, inc=1, device_id=to, device_id_type=pl.DeviceIdType.MESH)

    def greet_group(i, carry):
        greet((tm, lax.rem(tile + i, TILES)))
        return carry

    lax.fori_loop(1, TILES, greet_group, 0)
    for to in near:
        greet(to)

    w2[:, CMID:] = jnp.zeros((27, PAD - CMID, CMID), BF16)
    for d in range(3):
        spare = slice(d * PAD + CMID, (d + 1) * PAD)
        x2[:, :, :, spare] = jnp.zeros((6, 8, COLS, PAD - CMID), BF16)
        x3[:, :, :, spare] = jnp.zeros((FR, 6, COLS, PAD - CMID), BF16)
    lanes1[...] = member(CIN // GROUPS, False)
    chans1[...] = member(CIN // GROUPS, True)
    lanes2[...] = member(CMID // GROUPS, False)
    chans2[...] = member(CMID // GROUPS, True)

    loads[0].wait()
    sums, squares = [], []
    for f in range(FR):
        v = xraw[2 + f, 1:5].astype(F32).reshape(ROWS * COLS, CIN)
        sums.append(jnp.sum(v, axis=0, keepdims=True))
        squares.append(jnp.sum(v * v, axis=0, keepdims=True))
    mine[...] = partial_stats(jnp.concatenate(sums), jnp.concatenate(squares), lanes1[...])
    loads[4].wait()
    for a in range(2):
        for tap in range(2):
            if a == 0:
                q = [rkv[0, d].astype(F32) for d in range(3)] if tap == 0 else [
                    rkv[1, d].astype(F32) + rkv[2, d].astype(F32) for d in range(3)
                ]
            else:
                q = [rkv[0, d].astype(F32) + rkv[1, d].astype(F32) for d in range(3)] if tap == 0 else [
                    rkv[2, d].astype(F32) for d in range(3)
                ]
            none = jnp.zeros_like(q[0])
            cols = [
                jnp.concatenate([q[0], none], axis=1),
                jnp.concatenate([q[1] + q[2], q[0] + q[1]], axis=1),
                jnp.concatenate([none, q[2]], axis=1),
            ]
            for d in range(3):
                wres[a, tap, d * PAD : d * PAD + CMID] = cols[d].astype(BF16)
                wres[a, tap, d * PAD + CMID : (d + 1) * PAD] = jnp.zeros((PAD - CMID, 2 * COUT), BF16)

    loads[1].wait()
    pl.semaphore_wait(barrier, TILES - 1 + len(near))

    def exchange(src, at_in, phase):
        for far in range(8, 0, -1):
            for i in (far, TILES - far)[: 2 if far < 8 else 1]:
                remote(
                    src, at_in.at[i - 1], stat_s.at[phase, 0], stat_r.at[phase, 0],
                    (tm, lax.rem(tile + i, TILES)),
                ).start()

    def exchange_copy(at_in, phase):
        return remote(at_in, at_in, stat_s.at[phase, 0], stat_r.at[phase, 0], partner)

    def relay(total, at_prev, phase):
        return remote(total, at_prev, stat_s.at[phase, 1], stat_r.at[phase, 1], (tm_next, tile))

    def halo_copies(ref, rim, phase):
        lo, hi = rim, rim + ROWS
        head, tail = (lo, lo + rim), (hi - rim, hi)
        cuts = [
            ((2, 6), head, (2, 6), (hi, hi + rim), (tm, up)),
            ((2, 6), tail, (2, 6), (0, rim), (tm, down)),
            ((4, 6), (lo, hi), (0, 2), (lo, hi), (tm_next, tile)),
            ((4, 6), head, (0, 2), (hi, hi + rim), (tm_next, up)),
            ((4, 6), tail, (0, 2), (0, rim), (tm_next, down)),
        ]
        return [
            remote(
                ref.at[a[0] : a[1], b[0] : b[1]], ref.at[c[0] : c[1], d[0] : d[1]],
                halo_s.at[phase, i], halo_r.at[phase, i], to,
            )
            for i, (a, b, c, d, to) in enumerate(cuts)
        ]

    pair = remote(fk_in, fk_pair, pair_s.at[0], pair_r.at[0], partner)
    pair.start()
    exchange(mine, st_in, 0)

    pair.wait_recv()

    def unit_ref(u):
        if XT <= u < XT + YT:
            return wy.at[(u - XT) // YU, (u - XT) % YU]
        return w1.at[u]

    def both_halves(t):
        a, b = fk_in[t].astype(F32), fk_pair[t].astype(F32)
        return jnp.concatenate([jnp.where(core == 1, b, a), jnp.where(core == 1, a, b)], axis=0)

    for p in range(14):
        even = both_halves(2 * p)
        unit_ref(3 * p)[z] = even[:, :128].astype(BF16)
        if p < 13:
            odd = both_halves(2 * p + 1)
            unit_ref(3 * p + 1)[z] = odd[:, :128].astype(BF16)
            rest = jnp.concatenate([even[:, 128:], odd[:, 128:]], axis=1)
            unit_ref(3 * p + 2)[z] = rest.astype(BF16)
        else:
            rest = jnp.concatenate([even[:, 128:], jnp.zeros_like(even[:, 128:])], axis=1)
            unit_ref(3 * p + 1)[z] = rest.astype(BF16)

    my_x = XU * x
    blocks = 4

    def chip_of(k):
        return lax.rem(z - step * (k + 1) + 2 * NZ, NZ)

    def region(unit, count, chip, half):
        first = (count + 1) // 2
        if half is not None:
            unit, count = (unit, first) if half == 0 else (unit + first, count - first)
        return w1.at[pl.ds(unit, count), chip]

    def y_region(at, chip, half):
        return wy.at[at, :, chip] if half is None else wy.at[at, half, chip]

    def halves(k, body):
        if k < blocks - 1:
            body(None)
        else:
            for half in (0, 1):
                pl.when(core == half)(functools.partial(body, half))

    def z_copy(k, c, half):
        if c < 2:
            ref = region(my_x, XU, z, half) if c == 0 else y_region(y, z, half)
            by = k + 1
        else:
            ref = region(XT + YT, ZT, z if k < 2 else chip_of(1), half)
            by = k + 1 if k < 2 else k - 1
        return remote(ref, ref, zs.at[k, c], zr.at[k, c], along_z(step * by))

    def x_copy(k, hop, half):
        unit = my_x if hop != 1 else XU * lax.rem(x - step + NX, NX)
        ref = region(unit, XU, chip_of(k), half)
        return remote(ref, ref, xs.at[k, hop], xr.at[k, hop], along_x((step, step, -step)[hop]))

    def y_copy(k, hop, half):
        origin = {2: -2 * step, 3: -2 * step, 6: 2 * step}.get(hop, 0)
        by = (step, 2 * step, step, 2 * step, -step, -2 * step, -step)[hop]
        ref = y_region(lax.rem(y + origin + NY, NY), chip_of(k), half)
        return remote(ref, ref, ys.at[k, hop], yr.at[k, hop], along_y(by))

    def p_copy(k, i, half):
        if i < 4:
            by = (-step, -2 * step, step, 0)[i]
            ref = region(XU * lax.rem(x + by + NX, NX), XU, chip_of(k), half)
        elif i == 5:
            ref = region(XT + YT, ZT, chip_of(k), half)
        else:
            ref = y_region(slice(None), chip_of(k), half)
        return remote(ref, ref, ps.at[k, i], pr.at[k, i], partner)

    def z_start():
        for c in (1, 0):
            for k in range(blocks):
                halves(k, lambda half: z_copy(k, c, half).start())
        for k in (1, 0):
            z_copy(k, 2, None).start()

    def zy_arrived(k):
        def body(half):
            z_copy(k, 1, half).wait_recv()
            for hop in (1, 5, 0, 4):
                y_copy(k, hop, half).start()

        halves(k, body)

    def zx_arrived(k):
        def body(half):
            z_copy(k, 0, half).wait_recv()
            x_copy(k, 0, half).start()
            x_copy(k, 2, half).start()
            p_copy(k, 3, half).start()

        halves(k, body)

    def zz_arrived(k):
        halves(k, lambda half: z_copy(k, 2, half).wait_recv())
        if k == 1:
            halves(3, lambda half: z_copy(3, 2, half).start())
            z_copy(2, 2, None).start()
        halves(k, lambda half: p_copy(k, 5, half).start())

    def y_arrived(k):
        def body(half):
            for hop in (0, 4):
                y_copy(k, hop, half).wait_recv()
            y_copy(k, 1, half).wait_recv()
            y_copy(k, 3, half).start()
            y_copy(k, 2, half).start()
            y_copy(k, 5, half).wait_recv()
            y_copy(k, 6, half).start()

        halves(k, body)

    def y_last(k):
        def body(half):
            for hop in (6, 2, 3):
                y_copy(k, hop, half).wait_recv()
            p_copy(k, 4, half).start()

        halves(k, body)

    def x_arrived(k, hop):
        def body(half):
            x_copy(k, hop, half).wait_recv()
            if hop == 0:
                x_copy(k, 1, half).start()
            p_copy(k, hop, half).start()

        halves(k, body)

    z_start()
    halos = halo_copies(xraw, 1, 0)
    for copy in halos:
        copy.start()

    starts_here = span_start(clips, tm)
    keep_prev = jnp.where(starts_here, 0.0, 1.0).astype(F32)
    keep_top = jnp.where(tile == 0, 0.0, 1.0).astype(F32)
    keep_bottom = jnp.where(tile == TILES - 1, 0.0, 1.0).astype(F32)

    def first_act(f, scale, shift):
        a = silu(xraw[f].astype(F32) * scale[None, None, :] + shift[None, None, :])
        if f < 2:
            a = a * keep_prev
        a = jnp.concatenate([a[0:1] * keep_top, a[1:5], a[5:6] * keep_bottom], axis=0)
        for d, part in enumerate(shifted(a)):
            x1[f, :, :, d * CIN : (d + 1) * CIN] = part.astype(BF16)

    zy_arrived(0)
    zy_arrived(1)
    zy_arrived(2)
    exchange_copy(st_in, 0).wait_recv()
    st_total[...] = jnp.sum(st_in[...], axis=0) + mine[...]
    relayed = relay(st_total, st_prev, 0)
    relayed.start()
    zx_arrived(0)
    zy_arrived(3)
    zx_arrived(1)
    y_arrived(0)
    zx_arrived(2)
    y_arrived(1)
    x_arrived(0, 0)
    x_arrived(0, 2)
    y_arrived(2)
    zx_arrived(3)
    x_arrived(1, 0)
    x_arrived(1, 2)
    zz_arrived(1)
    y_arrived(3)
    for copy in halos[:2]:
        copy.wait_recv()
    gain, bias = g1[...].reshape(1, CIN), b1[...].reshape(1, CIN)
    scale, shift = affine(st_total[...], gain, bias, CIN // GROUPS, chans1[...])
    first_act(2, scale[0], shift[0])
    first_act(3, scale[1], shift[1])
    x_arrived(2, 0)
    x_arrived(2, 2)
    y_last(0)
    zz_arrived(0)
    first_act(4, scale[2], shift[2])
    first_act(5, scale[3], shift[3])
    x_arrived(0, 1)
    y_last(1)
    x_arrived(3, 0)
    x_arrived(3, 2)
    relayed.wait_recv()
    for copy in halos[2:]:
        copy.wait_recv()
    scale, shift = affine(st_prev[...], gain, bias, CIN // GROUPS, chans1[...])
    first_act(0, scale[2], shift[2])
    y_last(2)
    x_arrived(1, 1)
    first_act(1, scale[3], shift[3])
    y_last(3)
    zz_arrived(3)
    x_arrived(2, 1)
    zz_arrived(2)
    x_arrived(3, 1)

    def partner_wait(parts):
        for k in range(blocks):
            for i in parts:
                halves(k, lambda half: p_copy(k, i, None if half is None else 1 - half).wait_recv())

    def tap_window(t):
        s, rest = divmod(t, 9)
        dy, dx = divmod(rest, 3)
        window = x1[s : s + FR, dy : dy + ROWS, :, dx * CIN : (dx + 1) * CIN]
        return window.reshape(FR * ROWS * COLS, CIN)

    def conv1(pairs, first):
        total = [None, None] if first else [acc_ref[0], acc_ref[1]]

        def operands(p, odd):
            rest = unit_ref(3 * p + (2 if p < 13 else 1))[...].reshape(CIN, 128)
            return tap_window(2 * p + odd), jnp.concatenate(
                [unit_ref(3 * p + odd)[...].reshape(CIN, 128), rest], axis=1
            )

        for odd in range(2):
            taps = [operands(p, odd) for p in pairs if 2 * p + odd < 27]
            for at in range(0, len(taps), 2):
                window = jnp.concatenate([t[0] for t in taps[at : at + 2]], axis=1)
                weights = jnp.concatenate([t[1] for t in taps[at : at + 2]], axis=0)
                term = jnp.dot(window, weights, preferred_element_type=F32)
                total[odd] = term if total[odd] is None else total[odd] + term
        acc_ref[0], acc_ref[1] = total

    partner_wait((4, 5))
    conv1(range(6, 14), True)
    partner_wait((0, 1, 2, 3))
    conv1(range(0, 6), False)

    even, odd = acc_ref[0], acc_ref[1]
    hidden = jnp.concatenate([even[:, :128] + odd[:, :128], even[:, 128:192] + odd[:, 192:]], axis=1)
    hidden = hidden.reshape(FR, ROWS * COLS, CMID)
    mine2[...] = partial_stats(jnp.sum(hidden, axis=1), jnp.sum(hidden * hidden, axis=1), lanes2[...])
    exchange(mine2, st_in2, 1)
    hidden = hidden.reshape(FR, ROWS, COLS, CMID)
    hown[...] = hidden
    hraw[2:6, 2:6] = hidden.astype(BF16)
    halos2 = halo_copies(hraw, 2, 1)
    for copy in halos2:
        copy.start()

    loads[3].wait()
    loads[2].wait()
    acc2[...] = lax.dot_general(
        xraw[2:6].reshape(FR * 6 * COLS, CIN), wskip[...], (((1,), (1,)), ((), ())),
        preferred_element_type=F32,
    )

    exchange_copy(st_in2, 1).wait_recv()
    st_total2[...] = jnp.sum(st_in2[...], axis=0) + mine2[...]
    relayed2 = relay(st_total2, st_prev2, 1)
    relayed2.start()
    for copy in halos2[:2]:
        copy.wait_recv()

    def second_act(f, scale, shift):
        if f >= 2:
            v = jnp.concatenate(
                [hraw[f, 0:2].astype(F32), hown[f - 2], hraw[f, 6:8].astype(F32)], axis=0
            )
        else:
            v = hraw[f].astype(F32)
        a = silu(v * scale[None, None, :] + shift[None, None, :])
        if f < 2:
            a = a * keep_prev
        a = jnp.concatenate([a[0:2] * keep_top, a[2:6], a[6:8] * keep_bottom], axis=0)
        for d, part in enumerate(shifted(a)):
            x2[f, :, :, d * PAD : d * PAD + CMID] = part.astype(BF16)

    def conv2(frames, taps, total):
        for s in taps:
            for dy in range(3):
                window = x2[frames + s : frames + s + 2, dy : dy + 6].reshape(2 * 6 * COLS, 3 * PAD)
                weights = w2[9 * s + 3 * dy : 9 * s + 3 * dy + 3].reshape(3 * PAD, CMID)
                total = total + jnp.dot(window, weights, preferred_element_type=F32)
        return total

    def finish(frames, total):
        block = total.astype(BF16).astype(F32).reshape(2, 6, COLS, CMID)
        for f in range(2):
            a = jnp.concatenate(
                [block[f, 0:1] * keep_top, block[f, 1:5], block[f, 5:6] * keep_bottom], axis=0
            )
            for d, part in enumerate(shifted(a)):
                x3[frames + f, :, :, d * PAD : d * PAD + CMID] = part.astype(BF16)
        for a in range(2):
            res = None
            for tap in range(2):
                window = x3[frames : frames + 2, a + tap : a + tap + ROWS].reshape(2 * ROWS * COLS, 3 * PAD)
                term = jnp.dot(window, wres[a, tap], preferred_element_type=F32)
                res = term if res is None else res + term
            out_v[frames : frames + 2, :, a] = res.astype(BF16).reshape(2, ROWS, COLS, 2 * COUT)
        store = pltpu.make_async_copy(
            out_v.at[frames : frames + 2], out.at[frames : frames + 2], load_sem.at[5 + frames // 2]
        )
        store.start()
        return store

    two = 2 * 6 * COLS
    gain, bias = g2[...].reshape(1, CMID), b2[...].reshape(1, CMID)
    scale, shift = affine(st_total2[...], gain, bias, CMID // GROUPS, chans2[...])
    for f in range(FR):
        second_act(2 + f, scale[f], shift[f])
    stores = [finish(2, conv2(2, (0, 1, 2), acc2[two:]))]
    acc2[:two] = conv2(0, (2,), acc2[:two])
    relayed2.wait_recv()
    for copy in halos2[2:]:
        copy.wait_recv()
    scale, shift = affine(st_prev2[...], gain, bias, CMID // GROUPS, chans2[...])
    second_act(0, scale[2], shift[2])
    second_act(1, scale[3], shift[3])
    stores.append(finish(0, conv2(0, (0, 1), acc2[:two])))

    pair.wait_send()
    for copy in halos + halos2:
        copy.wait_send()
    for copy in (exchange_copy(st_in, 0), exchange_copy(st_in2, 1), relayed, relayed2):
        copy.wait_send()

    def drain(k, half):
        for c in range(3):
            z_copy(k, c, half).wait_send()
        for hop in range(3):
            x_copy(k, hop, half).wait_send()
        for hop in range(7):
            y_copy(k, hop, half).wait_send()
        for i in range(6):
            p_copy(k, i, half).wait_send()

    for k in range(blocks):
        halves(k, functools.partial(drain, k))
    for store in stores:
        store.wait()


def span_start(clips, tm):
    start, hit = jnp.int32(0), tm == 0
    for j in range(3):
        start = start + clips[j]
        hit = hit | (start == tm)
    return hit


def shards(
    latents, first_gain, first_bias, first_kernel, second_gain, second_bias,
    second_kernel, skip_weight, resample_kernel, clip_spans,
):
    fk = jnp.transpose(first_kernel, (1, 2, 3, 0, 4)).reshape(27, SHARD, CMID)
    sk = jnp.transpose(second_kernel, (1, 2, 3, 0, 4)).reshape(27, CMID, CMID)
    anywhere = pl.BlockSpec(memory_space=pl.ANY)
    vmem = pl.BlockSpec(memory_space=pltpu.VMEM)
    smem = pl.BlockSpec(memory_space=pltpu.SMEM)
    dma = pltpu.SemaphoreType.DMA
    out = pl.pallas_call(
        kernel,
        out_shape=jax.ShapeDtypeStruct((FR, ROWS, 2, COLS, 2 * COUT), BF16),
        in_specs=[anywhere, vmem, vmem, anywhere, vmem, vmem, anywhere, anywhere, anywhere, smem],
        out_specs=anywhere,
        scratch_shapes=[
            pltpu.VMEM((6, 6, COLS, CIN), BF16),
            pltpu.VMEM((27, SHARD, CMID), BF16),
            pltpu.VMEM((27, SHARD, CMID), BF16),
            pltpu.VMEM((UNITS, NZ, UNIT, 128), BF16),
            pltpu.VMEM((NY, YU, NZ, UNIT, 128), BF16),
            pltpu.VMEM((27, PAD, CMID), BF16),
            pltpu.VMEM((CMID, CIN), BF16),
            pltpu.VMEM((3, 3, CMID, COUT), BF16),
            pltpu.VMEM((6, 6, COLS, 3 * CIN), BF16),
            pltpu.VMEM((FR, ROWS, COLS, CMID), F32),
            pltpu.VMEM((6, 8, COLS, CMID), BF16),
            pltpu.VMEM((6, 8, COLS, 3 * PAD), BF16),
            pltpu.VMEM((FR, 6, COLS, 3 * PAD), BF16),
            pltpu.VMEM((2, 2, 3 * PAD, 2 * COUT), BF16),
            pltpu.VMEM((2, FR * ROWS * COLS, 256), F32),
            pltpu.VMEM((FR, ROWS, 2, COLS, 2 * COUT), BF16),
            pltpu.VMEM((FR * 6 * COLS, CMID), F32),
            pltpu.VMEM((2, 128), F32),
            pltpu.VMEM((TILES - 1, 2, 128), F32),
            pltpu.VMEM((2, 128), F32),
            pltpu.VMEM((2, 128), F32),
            pltpu.VMEM((2, 128), F32),
            pltpu.VMEM((TILES - 1, 2, 128), F32),
            pltpu.VMEM((2, 128), F32),
            pltpu.VMEM((2, 128), F32),
            pltpu.VMEM((CIN, 128), BF16),
            pltpu.VMEM((128, CIN), BF16),
            pltpu.VMEM((CMID, 128), BF16),
            pltpu.VMEM((128, CMID), BF16),
            dma((7,)),
            dma((2, 5)), dma((2, 5)),
            dma((2, 2)), dma((2, 2)),
            dma((1,)), dma((1,)),
            dma((4, 3)), dma((4, 3)),
            dma((4, 3)), dma((4, 3)),
            dma((4, 7)), dma((4, 7)),
            dma((4, 6)), dma((4, 6)),
        ],
        compiler_params=pltpu.CompilerParams(
            collective_id=0, has_side_effects=True, vmem_limit_bytes=56 * 2**20
        ),
    )(
        latents, first_gain, first_bias, fk,
        second_gain, second_bias, sk, skip_weight.T,
        resample_kernel, clip_spans,
    )
    return out.reshape(FR, 2 * ROWS, COLS, 2 * COUT)


def solution(mesh):
    in_specs = (
        P("tm", "tile", None, None), P(), P(), P("tile", None, None, None, None),
        P(), P(), P(), P(), P(), P(),
    )
    return jax.shard_map(
        shards, mesh=mesh, in_specs=in_specs, out_specs=P("tm", "tile", None, None), check_vma=False
    )
```

```python
import functools

import jax
import jax.numpy as jnp
from jax import lax
from jax.experimental import pallas as pl
from jax.experimental.pallas import tpu as pltpu
from jax.sharding import PartitionSpec as P

GROUPS = 32
EPS = 1e-6
F32 = jnp.float32
BF16 = jnp.bfloat16

FR, ROWS, COLS = 4, 4, 16
CIN, CMID, COUT = 384, 192, 96
SPANS, TILES = 32, 16
NX, NY, NZ = 4, 8, 8
SHARD = CIN // TILES
UNIT = 2 * SHARD
UNITS = 41
XU, YU = 4, 2
XT, YT = XU * NX, YU * NY
ZT = UNITS - XT - YT
PAD = 256
HEIGHT = ROWS * TILES


def member(per, transposed):
    channels = per * GROUPS
    shape = (128, channels) if transposed else (channels, 128)
    lane = lax.broadcasted_iota(jnp.int32, shape, 0 if transposed else 1)
    chan = lax.broadcasted_iota(jnp.int32, shape, 1 if transposed else 0)
    first = jnp.bitwise_and(lane, GROUPS - 1) * per
    return jnp.where((chan >= first) & (chan < first + per), 1.0, 0.0).astype(BF16)


def frame_lanes(rows):
    lane = lax.broadcasted_iota(jnp.int32, (rows, 128), 1)
    row = lax.broadcasted_iota(jnp.int32, (rows, 128), 0)
    low = jnp.bitwise_and(row, FR - 1) * GROUPS
    return (lane >= low) & (lane < low + GROUPS)


def exact_dot(values, zero_one):
    rows = values.shape[0]
    high = values.astype(BF16).astype(F32)
    left = values - high
    middle = left.astype(BF16).astype(F32)
    terms = jnp.concatenate([high, middle, left - middle], axis=0).astype(BF16)
    wide = jnp.dot(terms, zero_one, preferred_element_type=F32)
    return wide[:rows] + wide[rows : 2 * rows] + wide[2 * rows :]


def partial_stats(sums, squares, to_lanes):
    wide = exact_dot(jnp.concatenate([sums, squares], axis=0), to_lanes)
    wide = jnp.where(frame_lanes(2 * FR), wide, 0.0)
    return jnp.concatenate(
        [jnp.sum(wide[:FR], axis=0, keepdims=True), jnp.sum(wide[FR:], axis=0, keepdims=True)], axis=0
    )


def affine(message, gain, bias, per, to_channels):
    entries = float(HEIGHT * COLS * per)
    mean = message[0:1] / entries
    inv = lax.rsqrt(message[1:2] / entries - mean * mean + EPS)
    stacked = jnp.concatenate([jnp.broadcast_to(mean, (FR, 128)), jnp.broadcast_to(inv, (FR, 128))], axis=0)
    wide = exact_dot(jnp.where(frame_lanes(2 * FR), stacked, 0.0), to_channels)
    scale = wide[FR:] * gain
    return scale, bias - wide[:FR] * scale


def silu(v):
    half = 0.5 * v
    return half + half * jnp.tanh(half)


def shifted(a):
    zero = jnp.zeros(a.shape[:1] + (1,) + a.shape[2:], a.dtype)
    left = jnp.concatenate([zero, a[:, : COLS - 1]], axis=1)
    right = jnp.concatenate([a[:, 1:], zero], axis=1)
    return left, a, right


def kernel(
    lat, g1_in, b1_in, fk, g2_in, b2_in, sk, skw, rk, clips_in, out,
    clips, g1, b1, g2, b2, xraw, fk_in, fk_pair, w1, wy, w2, wskip, rkv, x1, hown, hraw, x2, x3, wres, acc_ref, acc2,
    mine, st_in, st_total, st_prev, mine2, st_in2, st_total2, st_prev2,
    lanes1, chans1, lanes2, chans2,
    load_sem, halo_s, halo_r, stat_s, stat_r, pair_s, pair_r,
    zs, zr, xs, xr, ys, yr, ps, pr,
):
    tm = lax.axis_index("tm")
    tile = lax.axis_index("tile")
    y, x = tm // NX, lax.rem(tm, NX)
    z, core = tile // 2, lax.rem(tile, 2)
    step = 1 - 2 * core
    tm_next, tm_prev = lax.rem(tm + 1, SPANS), lax.rem(tm + SPANS - 1, SPANS)
    up, down = lax.rem(tile + TILES - 1, TILES), lax.rem(tile + 1, TILES)
    partner = (tm, tile + step)

    def along_x(by):
        return (y * NX + lax.rem(x + by + 2 * NX, NX), tile)

    def along_y(by):
        return (lax.rem(y + by + 2 * NY, NY) * NX + x, tile)

    def along_z(by):
        return (tm, lax.rem(z + by + 2 * NZ, NZ) * 2 + core)

    def remote(src, dst, send, recv, to):
        return pltpu.make_async_remote_copy(
            src_ref=src, dst_ref=dst, send_sem=send, recv_sem=recv,
            device_id=to, device_id_type=pl.DeviceIdType.MESH,
        )

    loads = [
        pltpu.make_async_copy(lat, xraw.at[2:6, 1:5], load_sem.at[0]),
        pltpu.make_async_copy(fk, fk_in, load_sem.at[1]),
        pltpu.make_async_copy(sk, w2.at[:, :CMID], load_sem.at[2]),
        pltpu.make_async_copy(skw, wskip, load_sem.at[3]),
        pltpu.make_async_copy(rk, rkv, load_sem.at[4]),
        pltpu.make_async_copy(g1_in, g1, load_sem.at[5]),
        pltpu.make_async_copy(b1_in, b1, load_sem.at[6]),
        pltpu.make_async_copy(g2_in, g2, load_sem.at[7]),
        pltpu.make_async_copy(b2_in, b2, load_sem.at[8]),
        pltpu.make_async_copy(clips_in, clips, load_sem.at[9]),
    ]
    for load in loads:
        load.start()

    barrier = pltpu.get_barrier_semaphore()
    near = [along_x(1), along_x(-1), along_y(1), along_y(-1), along_y(2), along_y(-2)]
    near += [(tm_prev, tile), (tm_prev, up), (tm_prev, down)]

    def greet(to):
        pl.semaphore_signal(barrier, inc=1, device_id=to, device_id_type=pl.DeviceIdType.MESH)

    def greet_group(i, carry):
        greet((tm, lax.rem(tile + i, TILES)))
        return carry

    lax.fori_loop(1, TILES, greet_group, 0)
    for to in near:
        greet(to)

    w2[:, CMID:] = jnp.zeros((27, PAD - CMID, CMID), BF16)
    for d in range(3):
        spare = slice(d * PAD + CMID, (d + 1) * PAD)
        x2[:, :, :, spare] = jnp.zeros((6, 8, COLS, PAD - CMID), BF16)
        x3[:, :, :, spare] = jnp.zeros((FR, 6, COLS, PAD - CMID), BF16)
    lanes1[...] = member(CIN // GROUPS, False)
    chans1[...] = member(CIN // GROUPS, True)
    lanes2[...] = member(CMID // GROUPS, False)
    chans2[...] = member(CMID // GROUPS, True)

    loads[0].wait()
    sums, squares = [], []
    for f in range(FR):
        v = xraw[2 + f, 1:5].astype(F32).reshape(ROWS * COLS, CIN)
        sums.append(jnp.sum(v, axis=0, keepdims=True))
        squares.append(jnp.sum(v * v, axis=0, keepdims=True))
    mine[...] = partial_stats(jnp.concatenate(sums), jnp.concatenate(squares), lanes1[...])
    loads[4].wait()
    for a in range(2):
        for tap in range(2):
            if a == 0:
                q = [rkv[0, d].astype(F32) for d in range(3)] if tap == 0 else [
                    rkv[1, d].astype(F32) + rkv[2, d].astype(F32) for d in range(3)
                ]
            else:
                q = [rkv[0, d].astype(F32) + rkv[1, d].astype(F32) for d in range(3)] if tap == 0 else [
                    rkv[2, d].astype(F32) for d in range(3)
                ]
            none = jnp.zeros_like(q[0])
            cols = [
                jnp.concatenate([q[0], none], axis=1),
                jnp.concatenate([q[1] + q[2], q[0] + q[1]], axis=1),
                jnp.concatenate([none, q[2]], axis=1),
            ]
            for d in range(3):
                wres[a, tap, d * PAD : d * PAD + CMID] = cols[d].astype(BF16)
                wres[a, tap, d * PAD + CMID : (d + 1) * PAD] = jnp.zeros((PAD - CMID, 2 * COUT), BF16)

    for load in (loads[1], *loads[5:]):
        load.wait()
    pl.semaphore_wait(barrier, TILES - 1 + len(near))

    def exchange(src, at_in, phase):
        for far in range(8, 0, -1):
            for i in (far, TILES - far)[: 2 if far < 8 else 1]:
                remote(
                    src, at_in.at[i - 1], stat_s.at[phase, 0], stat_r.at[phase, 0],
                    (tm, lax.rem(tile + i, TILES)),
                ).start()

    def exchange_copy(at_in, phase):
        return remote(at_in, at_in, stat_s.at[phase, 0], stat_r.at[phase, 0], partner)

    def relay(total, at_prev, phase):
        return remote(total, at_prev, stat_s.at[phase, 1], stat_r.at[phase, 1], (tm_next, tile))

    def halo_copies(ref, rim, phase):
        lo, hi = rim, rim + ROWS
        head, tail = (lo, lo + rim), (hi - rim, hi)
        cuts = [
            ((2, 6), head, (2, 6), (hi, hi + rim), (tm, up)),
            ((2, 6), tail, (2, 6), (0, rim), (tm, down)),
            ((4, 6), (lo, hi), (0, 2), (lo, hi), (tm_next, tile)),
            ((4, 6), head, (0, 2), (hi, hi + rim), (tm_next, up)),
            ((4, 6), tail, (0, 2), (0, rim), (tm_next, down)),
        ]
        return [
            remote(
                ref.at[a[0] : a[1], b[0] : b[1]], ref.at[c[0] : c[1], d[0] : d[1]],
                halo_s.at[phase, i], halo_r.at[phase, i], to,
            )
            for i, (a, b, c, d, to) in enumerate(cuts)
        ]

    pair = remote(fk_in, fk_pair, pair_s.at[0], pair_r.at[0], partner)
    pair.start()
    exchange(mine, st_in, 0)

    pair.wait_recv()

    def unit_ref(u):
        if XT <= u < XT + YT:
            return wy.at[(u - XT) // YU, (u - XT) % YU]
        return w1.at[u]

    def both_halves(t):
        a, b = fk_in[t].astype(F32), fk_pair[t].astype(F32)
        return jnp.concatenate([jnp.where(core == 1, b, a), jnp.where(core == 1, a, b)], axis=0)

    for p in range(14):
        even = both_halves(2 * p)
        unit_ref(3 * p)[z] = even[:, :128].astype(BF16)
        if p < 13:
            odd = both_halves(2 * p + 1)
            unit_ref(3 * p + 1)[z] = odd[:, :128].astype(BF16)
            rest = jnp.concatenate([even[:, 128:], odd[:, 128:]], axis=1)
            unit_ref(3 * p + 2)[z] = rest.astype(BF16)
        else:
            rest = jnp.concatenate([even[:, 128:], jnp.zeros_like(even[:, 128:])], axis=1)
            unit_ref(3 * p + 1)[z] = rest.astype(BF16)

    my_x = XU * x
    blocks = 4

    def chip_of(k):
        return lax.rem(z - step * (k + 1) + 2 * NZ, NZ)

    def region(unit, count, chip, half):
        first = (count + 1) // 2
        if half is not None:
            unit, count = (unit, first) if half == 0 else (unit + first, count - first)
        return w1.at[pl.ds(unit, count), chip]

    def y_region(at, chip, half):
        return wy.at[at, :, chip] if half is None else wy.at[at, half, chip]

    def halves(k, body):
        if k < blocks - 1:
            body(None)
        else:
            for half in (0, 1):
                pl.when(core == half)(functools.partial(body, half))

    def z_copy(k, c, half):
        if c < 2:
            ref = region(my_x, XU, z, half) if c == 0 else y_region(y, z, half)
            by = k + 1
        else:
            ref = region(XT + YT, ZT, z if k < 2 else chip_of(1), half)
            by = k + 1 if k < 2 else k - 1
        return remote(ref, ref, zs.at[k, c], zr.at[k, c], along_z(step * by))

    def x_copy(k, hop, half):
        unit = my_x if hop != 1 else XU * lax.rem(x - step + NX, NX)
        ref = region(unit, XU, chip_of(k), half)
        return remote(ref, ref, xs.at[k, hop], xr.at[k, hop], along_x((step, step, -step)[hop]))

    def y_copy(k, hop, half):
        origin = {2: -2 * step, 3: -2 * step, 6: 2 * step}.get(hop, 0)
        by = (step, 2 * step, step, 2 * step, -step, -2 * step, -step)[hop]
        ref = y_region(lax.rem(y + origin + NY, NY), chip_of(k), half)
        return remote(ref, ref, ys.at[k, hop], yr.at[k, hop], along_y(by))

    def p_copy(k, i, half):
        if i < 4:
            by = (-step, -2 * step, step, 0)[i]
            ref = region(XU * lax.rem(x + by + NX, NX), XU, chip_of(k), half)
        elif i == 5:
            ref = region(XT + YT, ZT, chip_of(k), half)
        else:
            ref = y_region(slice(None), chip_of(k), half)
        return remote(ref, ref, ps.at[k, i], pr.at[k, i], partner)

    def z_start():
        for c in (1, 0):
            for k in range(blocks):
                halves(k, lambda half: z_copy(k, c, half).start())
        for k in (1, 0):
            z_copy(k, 2, None).start()

    def zy_arrived(k):
        def body(half):
            z_copy(k, 1, half).wait_recv()
            for hop in (1, 5, 0, 4):
                y_copy(k, hop, half).start()

        halves(k, body)

    def zx_arrived(k):
        def body(half):
            z_copy(k, 0, half).wait_recv()
            x_copy(k, 0, half).start()
            x_copy(k, 2, half).start()
            p_copy(k, 3, half).start()

        halves(k, body)

    def zz_arrived(k):
        halves(k, lambda half: z_copy(k, 2, half).wait_recv())
        if k == 1:
            halves(3, lambda half: z_copy(3, 2, half).start())
            z_copy(2, 2, None).start()
        halves(k, lambda half: p_copy(k, 5, half).start())

    def y_arrived(k):
        def body(half):
            for hop in (0, 4):
                y_copy(k, hop, half).wait_recv()
            y_copy(k, 1, half).wait_recv()
            y_copy(k, 3, half).start()
            y_copy(k, 2, half).start()
            y_copy(k, 5, half).wait_recv()
            y_copy(k, 6, half).start()

        halves(k, body)

    def y_last(k):
        def body(half):
            for hop in (6, 2, 3):
                y_copy(k, hop, half).wait_recv()
            p_copy(k, 4, half).start()

        halves(k, body)

    def x_arrived(k, hop):
        def body(half):
            x_copy(k, hop, half).wait_recv()
            if hop == 0:
                x_copy(k, 1, half).start()
            p_copy(k, hop, half).start()

        halves(k, body)

    z_start()
    halos = halo_copies(xraw, 1, 0)
    for copy in halos:
        copy.start()

    starts_here = span_start(clips, tm)
    keep_prev = jnp.where(starts_here, 0.0, 1.0).astype(F32)
    keep_top = jnp.where(tile == 0, 0.0, 1.0).astype(F32)
    keep_bottom = jnp.where(tile == TILES - 1, 0.0, 1.0).astype(F32)

    def first_act(f, scale, shift):
        a = silu(xraw[f].astype(F32) * scale[None, None, :] + shift[None, None, :])
        if f < 2:
            a = a * keep_prev
        a = jnp.concatenate([a[0:1] * keep_top, a[1:5], a[5:6] * keep_bottom], axis=0)
        for d, part in enumerate(shifted(a)):
            x1[f, :, :, d * CIN : (d + 1) * CIN] = part.astype(BF16)

    zy_arrived(0)
    zy_arrived(1)
    zy_arrived(2)
    exchange_copy(st_in, 0).wait_recv()
    st_total[...] = jnp.sum(st_in[...], axis=0) + mine[...]
    relayed = relay(st_total, st_prev, 0)
    relayed.start()
    zx_arrived(0)
    zy_arrived(3)
    zx_arrived(1)
    y_arrived(0)
    zx_arrived(2)
    y_arrived(1)
    x_arrived(0, 0)
    x_arrived(0, 2)
    y_arrived(2)
    zx_arrived(3)
    x_arrived(1, 0)
    x_arrived(1, 2)
    zz_arrived(1)
    y_arrived(3)
    for copy in halos[:2]:
        copy.wait_recv()
    gain, bias = g1[...].reshape(1, CIN), b1[...].reshape(1, CIN)
    scale, shift = affine(st_total[...], gain, bias, CIN // GROUPS, chans1[...])
    first_act(2, scale[0], shift[0])
    first_act(3, scale[1], shift[1])
    x_arrived(2, 0)
    x_arrived(2, 2)
    y_last(0)
    zz_arrived(0)
    first_act(4, scale[2], shift[2])
    first_act(5, scale[3], shift[3])
    x_arrived(0, 1)
    y_last(1)
    x_arrived(3, 0)
    x_arrived(3, 2)
    relayed.wait_recv()
    for copy in halos[2:]:
        copy.wait_recv()
    scale, shift = affine(st_prev[...], gain, bias, CIN // GROUPS, chans1[...])
    first_act(0, scale[2], shift[2])
    y_last(2)
    x_arrived(1, 1)
    first_act(1, scale[3], shift[3])
    y_last(3)
    zz_arrived(3)
    x_arrived(2, 1)
    zz_arrived(2)
    x_arrived(3, 1)

    def partner_wait(parts):
        for k in range(blocks):
            for i in parts:
                halves(k, lambda half: p_copy(k, i, None if half is None else 1 - half).wait_recv())

    def tap_window(t):
        s, rest = divmod(t, 9)
        dy, dx = divmod(rest, 3)
        window = x1[s : s + FR, dy : dy + ROWS, :, dx * CIN : (dx + 1) * CIN]
        return window.reshape(FR * ROWS * COLS, CIN)

    def conv1(pairs, first):
        total = [None, None] if first else [acc_ref[0], acc_ref[1]]

        def operands(p, odd):
            rest = unit_ref(3 * p + (2 if p < 13 else 1))[...].reshape(CIN, 128)
            return tap_window(2 * p + odd), jnp.concatenate(
                [unit_ref(3 * p + odd)[...].reshape(CIN, 128), rest], axis=1
            )

        for odd in range(2):
            taps = [operands(p, odd) for p in pairs if 2 * p + odd < 27]
            for at in range(0, len(taps), 2):
                window = jnp.concatenate([t[0] for t in taps[at : at + 2]], axis=1)
                weights = jnp.concatenate([t[1] for t in taps[at : at + 2]], axis=0)
                term = jnp.dot(window, weights, preferred_element_type=F32)
                total[odd] = term if total[odd] is None else total[odd] + term
        acc_ref[0], acc_ref[1] = total

    partner_wait((4, 5))
    conv1(range(6, 14), True)
    partner_wait((0, 1, 2, 3))
    conv1(range(0, 6), False)

    even, odd = acc_ref[0], acc_ref[1]
    hidden = jnp.concatenate([even[:, :128] + odd[:, :128], even[:, 128:192] + odd[:, 192:]], axis=1)
    hidden = hidden.reshape(FR, ROWS * COLS, CMID)
    mine2[...] = partial_stats(jnp.sum(hidden, axis=1), jnp.sum(hidden * hidden, axis=1), lanes2[...])
    exchange(mine2, st_in2, 1)
    hidden = hidden.reshape(FR, ROWS, COLS, CMID)
    hown[...] = hidden
    hraw[2:6, 2:6] = hidden.astype(BF16)
    halos2 = halo_copies(hraw, 2, 1)
    for copy in halos2:
        copy.start()

    loads[3].wait()
    loads[2].wait()
    acc2[...] = lax.dot_general(
        xraw[2:6].reshape(FR * 6 * COLS, CIN), wskip[...], (((1,), (1,)), ((), ())),
        preferred_element_type=F32,
    )

    exchange_copy(st_in2, 1).wait_recv()
    st_total2[...] = jnp.sum(st_in2[...], axis=0) + mine2[...]
    relayed2 = relay(st_total2, st_prev2, 1)
    relayed2.start()
    for copy in halos2[:2]:
        copy.wait_recv()

    def second_act(f, scale, shift):
        if f >= 2:
            v = jnp.concatenate(
                [hraw[f, 0:2].astype(F32), hown[f - 2], hraw[f, 6:8].astype(F32)], axis=0
            )
        else:
            v = hraw[f].astype(F32)
        a = silu(v * scale[None, None, :] + shift[None, None, :])
        if f < 2:
            a = a * keep_prev
        a = jnp.concatenate([a[0:2] * keep_top, a[2:6], a[6:8] * keep_bottom], axis=0)
        for d, part in enumerate(shifted(a)):
            x2[f, :, :, d * PAD : d * PAD + CMID] = part.astype(BF16)

    def conv2(frames, taps, total):
        for s in taps:
            for dy in range(3):
                window = x2[frames + s : frames + s + 2, dy : dy + 6].reshape(2 * 6 * COLS, 3 * PAD)
                weights = w2[9 * s + 3 * dy : 9 * s + 3 * dy + 3].reshape(3 * PAD, CMID)
                total = total + jnp.dot(window, weights, preferred_element_type=F32)
        return total

    def finish(frames, total):
        block = total.astype(BF16).astype(F32).reshape(2, 6, COLS, CMID)
        for f in range(2):
            a = jnp.concatenate(
                [block[f, 0:1] * keep_top, block[f, 1:5], block[f, 5:6] * keep_bottom], axis=0
            )
            for d, part in enumerate(shifted(a)):
                x3[frames + f, :, :, d * PAD : d * PAD + CMID] = part.astype(BF16)
        for a in range(2):
            res = None
            for tap in range(2):
                window = x3[frames : frames + 2, a + tap : a + tap + ROWS].reshape(2 * ROWS * COLS, 3 * PAD)
                term = jnp.dot(window, wres[a, tap], preferred_element_type=F32)
                res = term if res is None else res + term
            out[frames : frames + 2, :, a] = res.astype(BF16).reshape(2, ROWS, COLS, 2 * COUT)

    two = 2 * 6 * COLS
    gain, bias = g2[...].reshape(1, CMID), b2[...].reshape(1, CMID)
    scale, shift = affine(st_total2[...], gain, bias, CMID // GROUPS, chans2[...])
    for f in range(FR):
        second_act(2 + f, scale[f], shift[f])
    finish(2, conv2(2, (0, 1, 2), acc2[two:]))
    acc2[:two] = conv2(0, (2,), acc2[:two])
    relayed2.wait_recv()
    for copy in halos2[2:]:
        copy.wait_recv()
    scale, shift = affine(st_prev2[...], gain, bias, CMID // GROUPS, chans2[...])
    second_act(0, scale[2], shift[2])
    second_act(1, scale[3], shift[3])
    finish(0, conv2(0, (0, 1), acc2[:two]))

    pair.wait_send()
    for copy in halos + halos2:
        copy.wait_send()
    for copy in (exchange_copy(st_in, 0), exchange_copy(st_in2, 1), relayed, relayed2):
        copy.wait_send()

    def drain(k, half):
        for c in range(3):
            z_copy(k, c, half).wait_send()
        for hop in range(3):
            x_copy(k, hop, half).wait_send()
        for hop in range(7):
            y_copy(k, hop, half).wait_send()
        for i in range(6):
            p_copy(k, i, half).wait_send()

    for k in range(blocks):
        halves(k, functools.partial(drain, k))


def span_start(clips, tm):
    start, hit = jnp.int32(0), tm == 0
    for j in range(3):
        start = start + clips[j]
        hit = hit | (start == tm)
    return hit


def shards(
    latents, first_gain, first_bias, first_kernel, second_gain, second_bias,
    second_kernel, skip_weight, resample_kernel, clip_spans,
):
    fk = jnp.transpose(first_kernel, (1, 2, 3, 0, 4)).reshape(27, SHARD, CMID)
    sk = jnp.transpose(second_kernel, (1, 2, 3, 0, 4)).reshape(27, CMID, CMID)
    in_hbm = pl.BlockSpec(memory_space=pltpu.HBM)
    vmem = pl.BlockSpec(memory_space=pltpu.VMEM)
    dma = pltpu.SemaphoreType.DMA
    operands = (
        latents, first_gain, first_bias, fk, second_gain, second_bias, sk, skip_weight.T, resample_kernel, clip_spans,
    )
    out = pl.pallas_call(
        kernel,
        out_shape=jax.ShapeDtypeStruct((FR, ROWS, 2, COLS, 2 * COUT), BF16),
        in_specs=[in_hbm] * len(operands),
        out_specs=vmem,
        scratch_shapes=[
            pltpu.SMEM((4,), jnp.int32),
            pltpu.VMEM((CIN,), F32), pltpu.VMEM((CIN,), F32),
            pltpu.VMEM((CMID,), F32), pltpu.VMEM((CMID,), F32),
            pltpu.VMEM((6, 6, COLS, CIN), BF16),
            pltpu.VMEM((27, SHARD, CMID), BF16),
            pltpu.VMEM((27, SHARD, CMID), BF16),
            pltpu.VMEM((UNITS, NZ, UNIT, 128), BF16),
            pltpu.VMEM((NY, YU, NZ, UNIT, 128), BF16),
            pltpu.VMEM((27, PAD, CMID), BF16),
            pltpu.VMEM((CMID, CIN), BF16),
            pltpu.VMEM((3, 3, CMID, COUT), BF16),
            pltpu.VMEM((6, 6, COLS, 3 * CIN), BF16),
            pltpu.VMEM((FR, ROWS, COLS, CMID), F32),
            pltpu.VMEM((6, 8, COLS, CMID), BF16),
            pltpu.VMEM((6, 8, COLS, 3 * PAD), BF16),
            pltpu.VMEM((FR, 6, COLS, 3 * PAD), BF16),
            pltpu.VMEM((2, 2, 3 * PAD, 2 * COUT), BF16),
            pltpu.VMEM((2, FR * ROWS * COLS, 256), F32),
            pltpu.VMEM((FR * 6 * COLS, CMID), F32),
            pltpu.VMEM((2, 128), F32),
            pltpu.VMEM((TILES - 1, 2, 128), F32),
            pltpu.VMEM((2, 128), F32),
            pltpu.VMEM((2, 128), F32),
            pltpu.VMEM((2, 128), F32),
            pltpu.VMEM((TILES - 1, 2, 128), F32),
            pltpu.VMEM((2, 128), F32),
            pltpu.VMEM((2, 128), F32),
            pltpu.VMEM((CIN, 128), BF16),
            pltpu.VMEM((128, CIN), BF16),
            pltpu.VMEM((CMID, 128), BF16),
            pltpu.VMEM((128, CMID), BF16),
            dma((10,)),
            dma((2, 5)), dma((2, 5)),
            dma((2, 2)), dma((2, 2)),
            dma((1,)), dma((1,)),
            dma((4, 3)), dma((4, 3)),
            dma((4, 3)), dma((4, 3)),
            dma((4, 7)), dma((4, 7)),
            dma((4, 6)), dma((4, 6)),
        ],
        compiler_params=pltpu.CompilerParams(
            collective_id=0, has_side_effects=True, vmem_limit_bytes=28 * 2**20
        ),
    )(*[pltpu.with_memory_space_constraint(operand, pltpu.HBM) for operand in operands])
    return out.reshape(FR, 2 * ROWS, COLS, 2 * COUT)


def solution(mesh):
    in_specs = (
        P("tm", "tile", None, None), P(), P(), P("tile", None, None, None, None),
        P(), P(), P(), P(), P(), P(),
    )
    return jax.shard_map(
        shards, mesh=mesh, in_specs=in_specs, out_specs=P("tm", "tile", None, None), check_vma=False
    )
```

```python
import functools

import jax
import jax.numpy as jnp
from jax import lax
from jax.experimental import pallas as pl
from jax.experimental.pallas import tpu as pltpu
from jax.sharding import PartitionSpec as P

GROUPS = 32
EPS = 1e-6
F32 = jnp.float32
BF16 = jnp.bfloat16

FR, ROWS, COLS = 4, 4, 16
CIN, CMID, COUT = 384, 192, 96
SPANS, TILES = 32, 16
NX, NY, NZ = 4, 8, 8
SHARD = CIN // TILES
UNIT = 2 * SHARD
UNITS = 41
XU, YU = 4, 2
XT, YT = XU * NX, YU * NY
ZT = UNITS - XT - YT
PAD = 256
HEIGHT = ROWS * TILES


FAR_FIRST = sorted(range(1, TILES), key=lambda i: -min(i, TILES - i))


def member(per, transposed):
    channels = per * GROUPS
    shape = (128, channels) if transposed else (channels, 128)
    lane = lax.broadcasted_iota(jnp.int32, shape, 0 if transposed else 1)
    chan = lax.broadcasted_iota(jnp.int32, shape, 1 if transposed else 0)
    first = jnp.bitwise_and(lane, GROUPS - 1) * per
    return jnp.where((chan >= first) & (chan < first + per), 1.0, 0.0).astype(BF16)


def frame_lanes(rows):
    lane = lax.broadcasted_iota(jnp.int32, (rows, 128), 1)
    row = lax.broadcasted_iota(jnp.int32, (rows, 128), 0)
    low = jnp.bitwise_and(row, FR - 1) * GROUPS
    return (lane >= low) & (lane < low + GROUPS)


def exact_dot(values, zero_one):
    rows = values.shape[0]
    high = values.astype(BF16).astype(F32)
    left = values - high
    middle = left.astype(BF16).astype(F32)
    terms = jnp.concatenate([high, middle, left - middle], axis=0).astype(BF16)
    wide = jnp.dot(terms, zero_one, preferred_element_type=F32)
    return wide[:rows] + wide[rows : 2 * rows] + wide[2 * rows :]


def partial_stats(sums, squares, to_lanes):
    wide = exact_dot(jnp.concatenate([sums, squares], axis=0), to_lanes)
    wide = jnp.where(frame_lanes(2 * FR), wide, 0.0)
    return jnp.concatenate(
        [jnp.sum(wide[:FR], axis=0, keepdims=True), jnp.sum(wide[FR:], axis=0, keepdims=True)], axis=0
    )


def affine(message, gain, bias, per, to_channels):
    entries = float(HEIGHT * COLS * per)
    mean = message[0:1] / entries
    inv = lax.rsqrt(message[1:2] / entries - mean * mean + EPS)
    stacked = jnp.concatenate([jnp.broadcast_to(mean, (FR, 128)), jnp.broadcast_to(inv, (FR, 128))], axis=0)
    wide = exact_dot(jnp.where(frame_lanes(2 * FR), stacked, 0.0), to_channels)
    scale = wide[FR:] * gain
    return scale, bias - wide[:FR] * scale


def silu(v):
    half = 0.5 * v
    return half + half * jnp.tanh(half)


def shifted(a):
    zero = jnp.zeros(a.shape[:1] + (1,) + a.shape[2:], a.dtype)
    left = jnp.concatenate([zero, a[:, : COLS - 1]], axis=1)
    right = jnp.concatenate([a[:, 1:], zero], axis=1)
    return left, a, right


def kernel(
    lat, g1_in, b1_in, fk, g2_in, b2_in, sk, skw, rk, clips_in, out,
    clips, g1, b1, g2, b2, xraw, fk_in, fk_pair, w1, wy, w2, wskip, rkv, x1, hown, hraw, x2, x3, wres, acc_ref, acc2,
    mine, st_in, st_total, st_prev, mine2, st_in2, st_total2, st_prev2,
    lanes1, chans1, lanes2, chans2,
    load_sem, halo_s, halo_r, stat_s, stat_r, pair_s, pair_r,
    zs, zr, xs, xr, ys, yr, ps, pr,
):
    tm = lax.axis_index("tm")
    tile = lax.axis_index("tile")
    y, x = tm // NX, lax.rem(tm, NX)
    z, core = tile // 2, lax.rem(tile, 2)
    step = 1 - 2 * core
    tm_next, tm_prev = lax.rem(tm + 1, SPANS), lax.rem(tm + SPANS - 1, SPANS)
    up, down = lax.rem(tile + TILES - 1, TILES), lax.rem(tile + 1, TILES)
    partner = (tm, tile + step)

    def along_x(by):
        return (y * NX + lax.rem(x + by + 2 * NX, NX), tile)

    def along_y(by):
        return (lax.rem(y + by + 2 * NY, NY) * NX + x, tile)

    def along_z(by):
        return (tm, lax.rem(z + by + 2 * NZ, NZ) * 2 + core)

    def remote(src, dst, send, recv, to):
        return pltpu.make_async_remote_copy(
            src_ref=src, dst_ref=dst, send_sem=send, recv_sem=recv,
            device_id=to, device_id_type=pl.DeviceIdType.MESH,
        )

    barrier = pltpu.get_barrier_semaphore()
    near = [along_x(1), along_x(-1), along_y(1), along_y(-1), along_y(2), along_y(-2)]
    near += [(tm_prev, tile), (tm_prev, up), (tm_prev, down)]

    def greet(to):
        pl.semaphore_signal(barrier, inc=1, device_id=to, device_id_type=pl.DeviceIdType.MESH)

    for i in FAR_FIRST:
        greet((tm, lax.rem(tile + i, TILES)))
    for to in near:
        greet(to)

    loads = [
        pltpu.make_async_copy(lat, xraw.at[2:6, 1:5], load_sem.at[0]),
        pltpu.make_async_copy(fk, fk_in, load_sem.at[1]),
        pltpu.make_async_copy(sk, w2.at[:, :CMID], load_sem.at[2]),
        pltpu.make_async_copy(skw, wskip, load_sem.at[3]),
        pltpu.make_async_copy(rk, rkv, load_sem.at[4]),
        pltpu.make_async_copy(g1_in, g1, load_sem.at[5]),
        pltpu.make_async_copy(b1_in, b1, load_sem.at[6]),
        pltpu.make_async_copy(g2_in, g2, load_sem.at[7]),
        pltpu.make_async_copy(b2_in, b2, load_sem.at[8]),
        pltpu.make_async_copy(clips_in, clips, load_sem.at[9]),
    ]
    for load in loads:
        load.start()

    w2[:, CMID:] = jnp.zeros((27, PAD - CMID, CMID), BF16)
    for d in range(3):
        spare = slice(d * PAD + CMID, (d + 1) * PAD)
        x2[:, :, :, spare] = jnp.zeros((6, 8, COLS, PAD - CMID), BF16)
        x3[:, :, :, spare] = jnp.zeros((FR, 6, COLS, PAD - CMID), BF16)
    lanes1[...] = member(CIN // GROUPS, False)
    chans1[...] = member(CIN // GROUPS, True)
    lanes2[...] = member(CMID // GROUPS, False)
    chans2[...] = member(CMID // GROUPS, True)

    loads[0].wait()
    sums, squares = [], []
    for f in range(FR):
        v = xraw[2 + f, 1:5].astype(F32).reshape(ROWS * COLS, CIN)
        sums.append(jnp.sum(v, axis=0, keepdims=True))
        squares.append(jnp.sum(v * v, axis=0, keepdims=True))
    mine[...] = partial_stats(jnp.concatenate(sums), jnp.concatenate(squares), lanes1[...])
    loads[4].wait()
    for a in range(2):
        for tap in range(2):
            if a == 0:
                q = [rkv[0, d].astype(F32) for d in range(3)] if tap == 0 else [
                    rkv[1, d].astype(F32) + rkv[2, d].astype(F32) for d in range(3)
                ]
            else:
                q = [rkv[0, d].astype(F32) + rkv[1, d].astype(F32) for d in range(3)] if tap == 0 else [
                    rkv[2, d].astype(F32) for d in range(3)
                ]
            none = jnp.zeros_like(q[0])
            cols = [
                jnp.concatenate([q[0], none], axis=1),
                jnp.concatenate([q[1] + q[2], q[0] + q[1]], axis=1),
                jnp.concatenate([none, q[2]], axis=1),
            ]
            for d in range(3):
                wres[a, tap, d * PAD : d * PAD + CMID] = cols[d].astype(BF16)
                wres[a, tap, d * PAD + CMID : (d + 1) * PAD] = jnp.zeros((PAD - CMID, 2 * COUT), BF16)

    for load in (loads[1], *loads[5:]):
        load.wait()
    pl.semaphore_wait(barrier, TILES - 1 + len(near))

    def exchange(src, at_in, phase):
        for i in FAR_FIRST:
            remote(
                src, at_in.at[i - 1], stat_s.at[phase, 0], stat_r.at[phase, 0],
                (tm, lax.rem(tile + i, TILES)),
            ).start()

    def exchange_copy(at_in, phase):
        return remote(at_in, at_in, stat_s.at[phase, 0], stat_r.at[phase, 0], partner)

    def relay(total, at_prev, phase):
        return remote(total, at_prev, stat_s.at[phase, 1], stat_r.at[phase, 1], (tm_next, tile))

    def halo_copies(ref, rim, phase):
        lo, hi = rim, rim + ROWS
        head, tail = (lo, lo + rim), (hi - rim, hi)
        cuts = [
            ((2, 6), head, (2, 6), (hi, hi + rim), (tm, up)),
            ((2, 6), tail, (2, 6), (0, rim), (tm, down)),
            ((4, 6), (lo, hi), (0, 2), (lo, hi), (tm_next, tile)),
            ((4, 6), head, (0, 2), (hi, hi + rim), (tm_next, up)),
            ((4, 6), tail, (0, 2), (0, rim), (tm_next, down)),
        ]
        return [
            remote(
                ref.at[a[0] : a[1], b[0] : b[1]], ref.at[c[0] : c[1], d[0] : d[1]],
                halo_s.at[phase, i], halo_r.at[phase, i], to,
            )
            for i, (a, b, c, d, to) in enumerate(cuts)
        ]

    pair = remote(fk_in, fk_pair, pair_s.at[0], pair_r.at[0], partner)
    pair.start()
    exchange(mine, st_in, 0)

    pair.wait_recv()

    def unit_ref(u):
        if XT <= u < XT + YT:
            return wy.at[(u - XT) // YU, (u - XT) % YU]
        return w1.at[u]

    def both_halves(t):
        a, b = fk_in[t].astype(F32), fk_pair[t].astype(F32)
        return jnp.concatenate([jnp.where(core == 1, b, a), jnp.where(core == 1, a, b)], axis=0)

    for p in range(14):
        even = both_halves(2 * p)
        unit_ref(3 * p)[z] = even[:, :128].astype(BF16)
        if p < 13:
            odd = both_halves(2 * p + 1)
            unit_ref(3 * p + 1)[z] = odd[:, :128].astype(BF16)
            rest = jnp.concatenate([even[:, 128:], odd[:, 128:]], axis=1)
            unit_ref(3 * p + 2)[z] = rest.astype(BF16)
        else:
            rest = jnp.concatenate([even[:, 128:], jnp.zeros_like(even[:, 128:])], axis=1)
            unit_ref(3 * p + 1)[z] = rest.astype(BF16)

    my_x = XU * x
    blocks = 4

    def chip_of(k):
        return lax.rem(z - step * (k + 1) + 2 * NZ, NZ)

    def region(unit, count, chip, half):
        first = (count + 1) // 2
        if half is not None:
            unit, count = (unit, first) if half == 0 else (unit + first, count - first)
        return w1.at[pl.ds(unit, count), chip]

    def y_region(at, chip, half):
        return wy.at[at, :, chip] if half is None else wy.at[at, half, chip]

    def halves(k, body):
        if k < blocks - 1:
            body(None)
        else:
            for half in (0, 1):
                pl.when(core == half)(functools.partial(body, half))

    def z_copy(k, c, half):
        if c < 2:
            ref = region(my_x, XU, z, half) if c == 0 else y_region(y, z, half)
            by = k + 1
        else:
            ref = region(XT + YT, ZT, z if k < 2 else chip_of(1), half)
            by = k + 1 if k < 2 else k - 1
        return remote(ref, ref, zs.at[k, c], zr.at[k, c], along_z(step * by))

    def x_copy(k, hop, half):
        unit = my_x if hop != 1 else XU * lax.rem(x - step + NX, NX)
        ref = region(unit, XU, chip_of(k), half)
        return remote(ref, ref, xs.at[k, hop], xr.at[k, hop], along_x((step, step, -step)[hop]))

    def y_copy(k, hop, half):
        origin = {2: -2 * step, 3: -2 * step, 6: 2 * step}.get(hop, 0)
        by = (step, 2 * step, step, 2 * step, -step, -2 * step, -step)[hop]
        ref = y_region(lax.rem(y + origin + NY, NY), chip_of(k), half)
        return remote(ref, ref, ys.at[k, hop], yr.at[k, hop], along_y(by))

    def p_copy(k, i, half):
        if i < 4:
            by = (-step, -2 * step, step, 0)[i]
            ref = region(XU * lax.rem(x + by + NX, NX), XU, chip_of(k), half)
        elif i == 5:
            ref = region(XT + YT, ZT, chip_of(k), half)
        else:
            ref = y_region(slice(None), chip_of(k), half)
        return remote(ref, ref, ps.at[k, i], pr.at[k, i], partner)

    def z_start():
        for c in (1, 0):
            for k in range(blocks):
                halves(k, lambda half: z_copy(k, c, half).start())
        for k in (1, 0):
            z_copy(k, 2, None).start()

    def zy_arrived(k):
        def body(half):
            z_copy(k, 1, half).wait_recv()
            for hop in (1, 5, 0, 4):
                y_copy(k, hop, half).start()

        halves(k, body)

    def zx_arrived(k):
        def body(half):
            z_copy(k, 0, half).wait_recv()
            x_copy(k, 0, half).start()
            x_copy(k, 2, half).start()
            p_copy(k, 3, half).start()

        halves(k, body)

    def zz_arrived(k):
        halves(k, lambda half: z_copy(k, 2, half).wait_recv())
        if k == 1:
            halves(3, lambda half: z_copy(3, 2, half).start())
            z_copy(2, 2, None).start()
        halves(k, lambda half: p_copy(k, 5, half).start())

    def y_arrived(k):
        def body(half):
            for hop in (0, 4):
                y_copy(k, hop, half).wait_recv()
            y_copy(k, 1, half).wait_recv()
            y_copy(k, 3, half).start()
            y_copy(k, 2, half).start()
            y_copy(k, 5, half).wait_recv()
            y_copy(k, 6, half).start()

        halves(k, body)

    def y_last(k):
        def body(half):
            for hop in (6, 2, 3):
                y_copy(k, hop, half).wait_recv()
            p_copy(k, 4, half).start()

        halves(k, body)

    def x_arrived(k, hop):
        def body(half):
            x_copy(k, hop, half).wait_recv()
            if hop == 0:
                x_copy(k, 1, half).start()
            p_copy(k, hop, half).start()

        halves(k, body)

    z_start()
    halos = halo_copies(xraw, 1, 0)
    for copy in halos:
        copy.start()

    starts_here = span_start(clips, tm)
    keep_prev = jnp.where(starts_here, 0.0, 1.0).astype(F32)
    keep_top = jnp.where(tile == 0, 0.0, 1.0).astype(F32)
    keep_bottom = jnp.where(tile == TILES - 1, 0.0, 1.0).astype(F32)

    def first_act(f, scale, shift):
        a = silu(xraw[f].astype(F32) * scale[None, None, :] + shift[None, None, :])
        if f < 2:
            a = a * keep_prev
        a = jnp.concatenate([a[0:1] * keep_top, a[1:5], a[5:6] * keep_bottom], axis=0)
        for d, part in enumerate(shifted(a)):
            x1[f, :, :, d * CIN : (d + 1) * CIN] = part.astype(BF16)

    zy_arrived(0)
    zy_arrived(1)
    zy_arrived(2)
    exchange_copy(st_in, 0).wait_recv()
    st_total[...] = jnp.sum(st_in[...], axis=0) + mine[...]
    relayed = relay(st_total, st_prev, 0)
    relayed.start()
    zx_arrived(0)
    zy_arrived(3)
    zx_arrived(1)
    y_arrived(0)
    zx_arrived(2)
    y_arrived(1)
    x_arrived(0, 0)
    x_arrived(0, 2)
    y_arrived(2)
    zx_arrived(3)
    x_arrived(1, 0)
    x_arrived(1, 2)
    zz_arrived(1)
    y_arrived(3)
    for copy in halos[:2]:
        copy.wait_recv()
    gain, bias = g1[...].reshape(1, CIN), b1[...].reshape(1, CIN)
    scale, shift = affine(st_total[...], gain, bias, CIN // GROUPS, chans1[...])
    first_act(2, scale[0], shift[0])
    first_act(3, scale[1], shift[1])
    x_arrived(2, 0)
    x_arrived(2, 2)
    y_last(0)
    zz_arrived(0)
    first_act(4, scale[2], shift[2])
    first_act(5, scale[3], shift[3])
    x_arrived(0, 1)
    y_last(1)
    x_arrived(3, 0)
    x_arrived(3, 2)
    relayed.wait_recv()
    for copy in halos[2:]:
        copy.wait_recv()
    scale, shift = affine(st_prev[...], gain, bias, CIN // GROUPS, chans1[...])
    first_act(0, scale[2], shift[2])
    y_last(2)
    x_arrived(1, 1)
    first_act(1, scale[3], shift[3])
    y_last(3)
    zz_arrived(3)
    x_arrived(2, 1)
    zz_arrived(2)
    x_arrived(3, 1)

    def partner_wait(parts):
        for k in range(blocks):
            for i in parts:
                halves(k, lambda half: p_copy(k, i, None if half is None else 1 - half).wait_recv())

    def tap_window(t):
        s, rest = divmod(t, 9)
        dy, dx = divmod(rest, 3)
        window = x1[s : s + FR, dy : dy + ROWS, :, dx * CIN : (dx + 1) * CIN]
        return window.reshape(FR * ROWS * COLS, CIN)

    def conv1(pairs, first):
        total = [None, None] if first else [acc_ref[0], acc_ref[1]]

        def operands(p, odd):
            rest = unit_ref(3 * p + (2 if p < 13 else 1))[...].reshape(CIN, 128)
            return tap_window(2 * p + odd), jnp.concatenate(
                [unit_ref(3 * p + odd)[...].reshape(CIN, 128), rest], axis=1
            )

        for odd in range(2):
            taps = [operands(p, odd) for p in pairs if 2 * p + odd < 27]
            for at in range(0, len(taps), 2):
                window = jnp.concatenate([t[0] for t in taps[at : at + 2]], axis=1)
                weights = jnp.concatenate([t[1] for t in taps[at : at + 2]], axis=0)
                term = jnp.dot(window, weights, preferred_element_type=F32)
                total[odd] = term if total[odd] is None else total[odd] + term
        acc_ref[0], acc_ref[1] = total

    partner_wait((4, 5))
    conv1(range(6, 14), True)
    partner_wait((0, 1, 2, 3))
    conv1(range(0, 6), False)

    even, odd = acc_ref[0], acc_ref[1]
    hidden = jnp.concatenate([even[:, :128] + odd[:, :128], even[:, 128:192] + odd[:, 192:]], axis=1)
    hidden = hidden.reshape(FR, ROWS * COLS, CMID)
    mine2[...] = partial_stats(jnp.sum(hidden, axis=1), jnp.sum(hidden * hidden, axis=1), lanes2[...])
    exchange(mine2, st_in2, 1)
    hidden = hidden.reshape(FR, ROWS, COLS, CMID)
    hown[...] = hidden
    hraw[2:6, 2:6] = hidden.astype(BF16)
    halos2 = halo_copies(hraw, 2, 1)
    for copy in halos2:
        copy.start()

    loads[3].wait()
    loads[2].wait()
    acc2[...] = lax.dot_general(
        xraw[2:6].reshape(FR * 6 * COLS, CIN), wskip[...], (((1,), (1,)), ((), ())),
        preferred_element_type=F32,
    )

    exchange_copy(st_in2, 1).wait_recv()
    st_total2[...] = jnp.sum(st_in2[...], axis=0) + mine2[...]
    relayed2 = relay(st_total2, st_prev2, 1)
    relayed2.start()
    for copy in halos2[:2]:
        copy.wait_recv()

    def second_act(f, scale, shift):
        if f >= 2:
            v = jnp.concatenate(
                [hraw[f, 0:2].astype(F32), hown[f - 2], hraw[f, 6:8].astype(F32)], axis=0
            )
        else:
            v = hraw[f].astype(F32)
        a = silu(v * scale[None, None, :] + shift[None, None, :])
        if f < 2:
            a = a * keep_prev
        a = jnp.concatenate([a[0:2] * keep_top, a[2:6], a[6:8] * keep_bottom], axis=0)
        for d, part in enumerate(shifted(a)):
            x2[f, :, :, d * PAD : d * PAD + CMID] = part.astype(BF16)

    def conv2(frames, taps, total):
        for s in taps:
            for dy in range(3):
                window = x2[frames + s : frames + s + 2, dy : dy + 6].reshape(2 * 6 * COLS, 3 * PAD)
                weights = w2[9 * s + 3 * dy : 9 * s + 3 * dy + 3].reshape(3 * PAD, CMID)
                total = total + jnp.dot(window, weights, preferred_element_type=F32)
        return total

    def finish(frames, total):
        block = total.astype(BF16).astype(F32).reshape(2, 6, COLS, CMID)
        for f in range(2):
            a = jnp.concatenate(
                [block[f, 0:1] * keep_top, block[f, 1:5], block[f, 5:6] * keep_bottom], axis=0
            )
            for d, part in enumerate(shifted(a)):
                x3[frames + f, :, :, d * PAD : d * PAD + CMID] = part.astype(BF16)
        for a in range(2):
            res = None
            for tap in range(2):
                window = x3[frames : frames + 2, a + tap : a + tap + ROWS].reshape(2 * ROWS * COLS, 3 * PAD)
                term = jnp.dot(window, wres[a, tap], preferred_element_type=F32)
                res = term if res is None else res + term
            out[frames : frames + 2, :, a] = res.astype(BF16).reshape(2, ROWS, COLS, 2 * COUT)

    two = 2 * 6 * COLS
    gain, bias = g2[...].reshape(1, CMID), b2[...].reshape(1, CMID)
    scale, shift = affine(st_total2[...], gain, bias, CMID // GROUPS, chans2[...])
    for f in range(FR):
        second_act(2 + f, scale[f], shift[f])
    finish(2, conv2(2, (0, 1, 2), acc2[two:]))
    acc2[:two] = conv2(0, (2,), acc2[:two])
    relayed2.wait_recv()
    for copy in halos2[2:]:
        copy.wait_recv()
    scale, shift = affine(st_prev2[...], gain, bias, CMID // GROUPS, chans2[...])
    second_act(0, scale[2], shift[2])
    second_act(1, scale[3], shift[3])
    finish(0, conv2(0, (0, 1), acc2[:two]))

    pair.wait_send()
    for copy in halos + halos2:
        copy.wait_send()
    for copy in (exchange_copy(st_in, 0), exchange_copy(st_in2, 1), relayed, relayed2):
        copy.wait_send()

    def drain(k, half):
        for c in range(3):
            z_copy(k, c, half).wait_send()
        for hop in range(3):
            x_copy(k, hop, half).wait_send()
        for hop in range(7):
            y_copy(k, hop, half).wait_send()
        for i in range(6):
            p_copy(k, i, half).wait_send()

    for k in range(blocks):
        halves(k, functools.partial(drain, k))


def span_start(clips, tm):
    start, hit = jnp.int32(0), tm == 0
    for j in range(3):
        start = start + clips[j]
        hit = hit | (start == tm)
    return hit


def shards(
    latents, first_gain, first_bias, first_kernel, second_gain, second_bias,
    second_kernel, skip_weight, resample_kernel, clip_spans,
):
    fk = jnp.transpose(first_kernel, (1, 2, 3, 0, 4)).reshape(27, SHARD, CMID)
    sk = jnp.transpose(second_kernel, (1, 2, 3, 0, 4)).reshape(27, CMID, CMID)
    in_hbm = pl.BlockSpec(memory_space=pltpu.HBM)
    vmem = pl.BlockSpec(memory_space=pltpu.VMEM)
    dma = pltpu.SemaphoreType.DMA
    operands = (
        latents, first_gain, first_bias, fk, second_gain, second_bias, sk, skip_weight.T, resample_kernel, clip_spans,
    )
    out = pl.pallas_call(
        kernel,
        out_shape=jax.ShapeDtypeStruct((FR, ROWS, 2, COLS, 2 * COUT), BF16),
        in_specs=[in_hbm] * len(operands),
        out_specs=vmem,
        scratch_shapes=[
            pltpu.SMEM((4,), jnp.int32),
            pltpu.VMEM((CIN,), F32), pltpu.VMEM((CIN,), F32),
            pltpu.VMEM((CMID,), F32), pltpu.VMEM((CMID,), F32),
            pltpu.VMEM((6, 6, COLS, CIN), BF16),
            pltpu.VMEM((27, SHARD, CMID), BF16),
            pltpu.VMEM((27, SHARD, CMID), BF16),
            pltpu.VMEM((UNITS, NZ, UNIT, 128), BF16),
            pltpu.VMEM((NY, YU, NZ, UNIT, 128), BF16),
            pltpu.VMEM((27, PAD, CMID), BF16),
            pltpu.VMEM((CMID, CIN), BF16),
            pltpu.VMEM((3, 3, CMID, COUT), BF16),
            pltpu.VMEM((6, 6, COLS, 3 * CIN), BF16),
            pltpu.VMEM((FR, ROWS, COLS, CMID), F32),
            pltpu.VMEM((6, 8, COLS, CMID), BF16),
            pltpu.VMEM((6, 8, COLS, 3 * PAD), BF16),
            pltpu.VMEM((FR, 6, COLS, 3 * PAD), BF16),
            pltpu.VMEM((2, 2, 3 * PAD, 2 * COUT), BF16),
            pltpu.VMEM((2, FR * ROWS * COLS, 256), F32),
            pltpu.VMEM((FR * 6 * COLS, CMID), F32),
            pltpu.VMEM((2, 128), F32),
            pltpu.VMEM((TILES - 1, 2, 128), F32),
            pltpu.VMEM((2, 128), F32),
            pltpu.VMEM((2, 128), F32),
            pltpu.VMEM((2, 128), F32),
            pltpu.VMEM((TILES - 1, 2, 128), F32),
            pltpu.VMEM((2, 128), F32),
            pltpu.VMEM((2, 128), F32),
            pltpu.VMEM((CIN, 128), BF16),
            pltpu.VMEM((128, CIN), BF16),
            pltpu.VMEM((CMID, 128), BF16),
            pltpu.VMEM((128, CMID), BF16),
            dma((10,)),
            dma((2, 5)), dma((2, 5)),
            dma((2, 2)), dma((2, 2)),
            dma((1,)), dma((1,)),
            dma((4, 3)), dma((4, 3)),
            dma((4, 3)), dma((4, 3)),
            dma((4, 7)), dma((4, 7)),
            dma((4, 6)), dma((4, 6)),
        ],
        compiler_params=pltpu.CompilerParams(
            collective_id=0, has_side_effects=True, vmem_limit_bytes=28 * 2**20
        ),
    )(*[pltpu.with_memory_space_constraint(operand, pltpu.HBM) for operand in operands])
    return out.reshape(FR, 2 * ROWS, COLS, 2 * COUT)


def solution(mesh):
    in_specs = (
        P("tm", "tile", None, None), P(), P(), P("tile", None, None, None, None),
        P(), P(), P(), P(), P(), P(),
    )
    return jax.shard_map(
        shards, mesh=mesh, in_specs=in_specs, out_specs=P("tm", "tile", None, None), check_vma=False
    )
```
